128 devices in a mesh: ctx: 16 (over y, x_hi, core), tp: 8 (over z, x_lo).
Axes of the slice: x: 4 (x_hi: 2, x_lo: 2; x = x_hi * 2 + x_lo), y: 4, z: 4, core: 2. Of those that a mesh axis runs over, the one named last changes fastest.
Arguments:
- tokens: bfloat16 [2, 2048, 4096], P(None, 'ctx', 'tp'), may hold values from -7 to 7
- w_query: bfloat16 [4096, 2048], P(None, 'tp'), may hold values from -0.09375 to 0.09375
- w_key: bfloat16 [4096, 2048], P(None, 'tp'), may hold values from -0.09375 to 0.09375
- w_value: bfloat16 [4096, 2048], P(None, 'tp'), may hold values from -0.09375 to 0.09375
- w_out: bfloat16 [2048, 4096], P('tp'), may hold values from -0.125 to 0.125
- allowed: int32 [2, 16, 16], P(None, 'ctx'), may hold values from 0 to 1, as said below
- grad_out: bfloat16 [2, 2048, 4096], P(None, 'ctx', 'tp'), may hold values from -6 to 6
Outputs:
- attended: bfloat16 [2, 2048, 4096], P(None, 'ctx', 'tp')
- grad_tokens: bfloat16 [2, 2048, 4096], P(None, 'ctx', 'tp')
- grad_query: bfloat16 [4096, 2048], P('ctx', 'tp')
- grad_key: bfloat16 [4096, 2048], P('ctx', 'tp')
- grad_value: bfloat16 [4096, 2048], P('ctx', 'tp')
- grad_out_proj: bfloat16 [2048, 4096], P('tp', 'ctx')
The draws below stay inside these ranges and needn't reach their ends.
Inputs may be any that keep to these rules, and one draw needn't show every extreme that they name: For each sequence b and query block i, allowed[b, i, j] is 1 exactly for j from some first block up to i: a block always sees itself and never a later block.
All inputs are finite; a program needn't handle non-finite values.
Results may differ from the reference program's by a relative error of at most 0.035.
Values may be sent and summed in bfloat16 or wider, within the bound.
A program may use at most 128 MiB of HBM per device.

```python
import jax
import jax.numpy as jnp
from jax import lax

D = 4096
HEADS = 16
HEAD_DIM = 128
BLK = 128
FRAME = 16
BATCH = 2
SEQ = 2048
HW = 2048
NBLK = 16


def shared_normal(key):
    return jnp.clip(jax.random.normal(key, (D, HW), jnp.float32), -4.0, 4.0)


def draw_w_query(key, part):
    common = shared_normal(key)
    key = jax.random.fold_in(key, 21)
    own = jnp.clip(jax.random.normal(key, (D, HW), jnp.float32), -4.0, 4.0)
    return ((0.8 * common + 0.6 * own) * D ** (-0.5)).astype(jnp.bfloat16)


def draw_w_key(key, part):
    common = shared_normal(key)
    key = jax.random.fold_in(key, 22)
    own = jnp.clip(jax.random.normal(key, (D, HW), jnp.float32), -4.0, 4.0)
    return ((0.8 * common + 0.6 * own) * D ** (-0.5)).astype(jnp.bfloat16)


def draw_tokens(key, part):
    key = jax.random.fold_in(key, 11)
    base_key = jax.random.fold_in(key, 0)
    return jnp.clip(jax.random.normal(base_key, (BATCH, SEQ, D), jnp.float32), -6.0, 6.0).astype(jnp.bfloat16)


def draw_allowed(key, part):
    key = jax.random.fold_in(key, 31)
    diagonal_index = jnp.arange(NBLK)
    first_block = jax.random.randint(key, (BATCH, NBLK), 0, diagonal_index + 1)
    column = jnp.arange(NBLK)
    inside = (column[None, None, :] >= first_block[:, :, None]) & (column[None, None, :] <= diagonal_index[None, :, None])
    return inside.astype(jnp.int32)


def spiked(entries, stream_key, source, target, shards_of, factor):
    def block_of(axis_at):
        return (jnp.arange(entries.shape[axis_at]) // (entries.shape[axis_at] // shards_of)).reshape((-1,) + (1,) * (entries.ndim - 1 - axis_at))

    near = jax.random.permutation(stream_key, shards_of)[block_of(target)]
    far = (block_of(target) + shards_of // 2) % shards_of
    return jnp.where((block_of(source) == near) | (block_of(source) == far), factor * entries, entries)


def block_scale(stream_key, dims, cuts, low, top_value):
    def one(dim, parts):
        draws = jax.random.uniform(jax.random.fold_in(jax.random.fold_in(stream_key, 6), dim), (parts,), jnp.float32, low / len(cuts), top_value / len(cuts))
        return jnp.repeat(jnp.exp(draws), dims[dim] // parts).reshape((-1,) + (1,) * (len(dims) - dim - 1))

    gain = one(*cuts[0])
    for cut in cuts[1:]:
        gain = gain * one(*cut)
    return gain


def scatter_about(own_key, dims, spread, most, cuts=(), dtype=jnp.bfloat16):
    gain = block_scale(own_key, dims, cuts, -0.22, 0.18) if cuts else 1.0
    result = jax.random.normal(own_key, dims, jnp.float32) * spread * gain
    return jnp.minimum(jnp.maximum(result, -most), most).astype(dtype)


def bell_draw_with(key, shape, deviation, bound, pieces, heavy, kind=jnp.bfloat16):
    result = deviation * jax.random.normal(key, shape, jnp.float32)
    if pieces:
        result = result * block_scale(key, shape, pieces, -0.22, 0.18)
    return jnp.clip(spiked(result, jax.random.fold_in(key, 3), *heavy), -bound, bound).astype(kind)


def setup_inputs(seed: int = 0) -> dict:
    streams_of = jax.random.split(jax.random.key(seed), 8)
    tokens = draw_tokens(jax.random.fold_in(streams_of[7], 71), 0)
    w_query = draw_w_query(jax.random.fold_in(streams_of[7], 71), 0)
    w_key = draw_w_key(jax.random.fold_in(streams_of[7], 71), 0)
    w_value = scatter_about(streams_of[3], (D, HW), D ** -0.5, 0.09375, ((1, 8),))
    w_out = scatter_about(streams_of[4], (HW, D), HW ** -0.5, 0.125, ((0, 8),))
    allowed = draw_allowed(jax.random.fold_in(streams_of[7], 71), 0)
    grad_out = bell_draw_with(streams_of[6], (BATCH, SEQ, D), 1.0, 6.0, ((1, 16), (2, 8)), (1, 2, 16, 2.0))
    return {"tokens": tokens, "w_query": w_query, "w_key": w_key, "w_value": w_value, "w_out": w_out, "allowed": allowed, "grad_out": grad_out}


def cast_half_precision(array):
    return lax.optimization_barrier(array.astype(jnp.bfloat16))


def visibility(allowed):
    position = jnp.arange(SEQ)
    block_of = position // BLK
    frame_of = position // FRAME
    blockwise = allowed[:, block_of][:, :, block_of] == 1
    return blockwise & (frame_of[None, None, :] <= frame_of[None, :, None])


def reference(tokens, w_query, w_key, w_value, w_out, allowed, grad_out):
    queries = cast_half_precision(jnp.dot(tokens, w_query, preferred_element_type=jnp.float32))
    key_rows = cast_half_precision(jnp.dot(tokens, w_key, preferred_element_type=jnp.float32))
    value_rows = cast_half_precision(jnp.dot(tokens, w_value, preferred_element_type=jnp.float32))
    grad_heads = cast_half_precision(jnp.dot(grad_out, w_out.T, preferred_element_type=jnp.float32))
    visible = visibility(allowed)
    logit_scale = HEAD_DIM ** -0.5

    def one_head(head_index):
        offset = head_index * HEAD_DIM
        queries_per_head = lax.dynamic_slice_in_dim(queries, offset, HEAD_DIM, 2).astype(jnp.float32)
        keys_per_head = lax.dynamic_slice_in_dim(key_rows, offset, HEAD_DIM, 2).astype(jnp.float32)
        values_per_head = lax.dynamic_slice_in_dim(value_rows, offset, HEAD_DIM, 2).astype(jnp.float32)
        head_gradient = lax.dynamic_slice_in_dim(grad_heads, offset, HEAD_DIM, 2).astype(jnp.float32)
        attention_logits = jnp.einsum("foj,fuj->fou", queries_per_head, keys_per_head) * logit_scale
        attention_logits = jnp.where(visible, attention_logits, -jnp.inf)
        exponent = jnp.exp(attention_logits - jnp.max(attention_logits, axis=2, keepdims=True))
        weights = exponent / jnp.sum(exponent, axis=2, keepdims=True)
        half_precision = cast_half_precision(weights).astype(jnp.float32)
        head_mixture = cast_half_precision(jnp.einsum("zhc,zcv->zhv", half_precision, values_per_head))
        weight_gradient = jnp.einsum("foj,fuj->fou", head_gradient, values_per_head)
        row_inner = jnp.sum(head_gradient * head_mixture.astype(jnp.float32), axis=2, keepdims=True)
        score_gradient = cast_half_precision(weights * (weight_gradient - row_inner) * logit_scale).astype(jnp.float32)
        query_gradient = jnp.einsum("zhc,zcv->zhv", score_gradient, keys_per_head)
        key_gradient = jnp.einsum("mjl,mjz->mlz", score_gradient, queries_per_head)
        value_gradient = jnp.einsum("mjl,mjz->mlz", half_precision, head_gradient)
        return (head_mixture, cast_half_precision(query_gradient), cast_half_precision(key_gradient), cast_half_precision(value_gradient))

    stacked = lax.map(one_head, jnp.arange(HEADS))

    def join_heads(array):
        return jnp.transpose(array, (1, 2, 0, 3)).reshape(BATCH, SEQ, HW)

    mixed_heads = join_heads(stacked[0])
    query_gradient = join_heads(stacked[1])
    key_gradient = join_heads(stacked[2])
    value_gradient = join_heads(stacked[3])
    attended = jnp.dot(mixed_heads, w_out, preferred_element_type=jnp.float32).astype(jnp.bfloat16)
    grad_tokens = (jnp.dot(query_gradient, w_query.T, preferred_element_type=jnp.float32)
                   + jnp.dot(key_gradient, w_key.T, preferred_element_type=jnp.float32)
                   + jnp.dot(value_gradient, w_value.T, preferred_element_type=jnp.float32)).astype(jnp.bfloat16)
    flat_tokens = tokens.reshape(BATCH * SEQ, D)
    flat_grads = grad_out.reshape(BATCH * SEQ, D)
    grad_query = jnp.dot(flat_tokens.T, query_gradient.reshape(BATCH * SEQ, HW), preferred_element_type=jnp.float32).astype(jnp.bfloat16)
    grad_key = jnp.dot(flat_tokens.T, key_gradient.reshape(BATCH * SEQ, HW), preferred_element_type=jnp.float32).astype(jnp.bfloat16)
    grad_value = jnp.dot(flat_tokens.T, value_gradient.reshape(BATCH * SEQ, HW), preferred_element_type=jnp.float32).astype(jnp.bfloat16)
    grad_out_proj = jnp.dot(mixed_heads.reshape(BATCH * SEQ, HW).T, flat_grads, preferred_element_type=jnp.float32).astype(jnp.bfloat16)
    return (attended, grad_tokens, grad_query, grad_key, grad_value, grad_out_proj)
```

```python
import jax
import jax.numpy as jnp
from jax import lax
from jax.sharding import PartitionSpec as P

HEAD_DIM = 128
FRAME = 16


def cast_half_precision(array):
    return array.astype(jnp.bfloat16)


def half_concatenate(pieces, axis):
    return jnp.concatenate([cast_half_precision(piece) for piece in pieces], axis=axis)


def per_device(tokens, w_query, w_key, w_value, w_out, allowed, grad_out):
    batch_size = tokens.shape[0]
    block_len = tokens.shape[1]
    head_width = w_query.shape[1]
    heads_here = head_width // HEAD_DIM
    cycle_index = lax.axis_index("ctx")
    full_tokens, full_grads = (
        lax.all_gather(tokens, "tp", axis=2, tiled=True),
        lax.all_gather(grad_out, "tp", axis=2, tiled=True),
    )
    queries = cast_half_precision(jnp.dot(full_tokens, w_query, preferred_element_type=jnp.float32))
    key_rows = cast_half_precision(jnp.dot(full_tokens, w_key, preferred_element_type=jnp.float32))
    value_rows = cast_half_precision(
        jnp.dot(full_tokens, w_value, preferred_element_type=jnp.float32)
    )
    all_keys, all_values = (
        lax.all_gather(key_rows, "ctx", axis=1, tiled=True),
        lax.all_gather(value_rows, "ctx", axis=1, tiled=True),
    )
    window_len = all_keys.shape[1]
    query_pos = cycle_index * block_len + jnp.arange(block_len)
    key_pos = jnp.arange(window_len)
    block_ok = jnp.repeat(allowed[:, 0, :], block_len, axis=1) == 1
    visible = block_ok[:, None, :] & (
        (key_pos // FRAME)[None, None, :] <= (query_pos // FRAME)[None, :, None]
    )
    logit_scale = HEAD_DIM ** (-0.5)
    split_queries = queries.reshape(batch_size, block_len, heads_here, HEAD_DIM)
    split_keys = all_keys.reshape(batch_size, window_len, heads_here, HEAD_DIM)
    split_values = all_values.reshape(batch_size, window_len, heads_here, HEAD_DIM)
    attention_logits = (
        jnp.einsum("bqhd,bkhd->bhqk", split_queries, split_keys, preferred_element_type=jnp.float32)
        * logit_scale
    )
    attention_logits = jnp.where(visible[:, None], attention_logits, -jnp.inf)
    row_max = jnp.max(attention_logits, axis=3, keepdims=True)
    exponent = jnp.exp(attention_logits - row_max)
    row_total = jnp.sum(exponent, axis=3, keepdims=True)
    weights = exponent / row_total
    half_precision = cast_half_precision(weights)
    split_mixed = cast_half_precision(
        jnp.einsum(
            "bhqk,bkhd->bqhd", half_precision, split_values, preferred_element_type=jnp.float32
        )
    )
    mixed_heads = split_mixed.reshape(batch_size, block_len, head_width)
    out_terms = jnp.dot(mixed_heads, w_out, preferred_element_type=jnp.float32)
    attended = lax.psum_scatter(
        cast_half_precision(out_terms), "tp", scatter_dimension=2, tiled=True
    )
    grad_heads = cast_half_precision(
        jnp.einsum("bqe,he->bqh", full_grads, w_out, preferred_element_type=jnp.float32)
    )
    split_grads = grad_heads.reshape(batch_size, block_len, heads_here, HEAD_DIM)
    back_keys = split_keys
    back_values = split_values
    weight_gradient = jnp.einsum(
        "bqhd,bkhd->bhqk", split_grads, back_values, preferred_element_type=jnp.float32
    )
    row_inner = jnp.einsum(
        "bqhd,bqhd->bhq", split_grads, split_mixed, preferred_element_type=jnp.float32
    )[..., None]
    score_gradient = cast_half_precision(weights * (weight_gradient - row_inner) * logit_scale)
    query_gradient = cast_half_precision(
        jnp.einsum("bhqk,bkhd->bqhd", score_gradient, back_keys, preferred_element_type=jnp.float32)
    ).reshape(batch_size, block_len, head_width)
    key_part = jnp.einsum(
        "bhqk,bqhd->kbhd", score_gradient, split_queries, preferred_element_type=jnp.float32
    )
    value_part = jnp.einsum(
        "bhqk,bqhd->kbhd", half_precision, split_grads, preferred_element_type=jnp.float32
    )
    key_value = lax.psum_scatter(
        half_concatenate(
            (
                key_part.reshape(block_len * lax.axis_size("ctx"), batch_size, head_width),
                value_part.reshape(block_len * lax.axis_size("ctx"), batch_size, head_width),
            ),
            axis=2,
        ),
        "ctx",
        scatter_dimension=0,
        tiled=True,
    )
    key_gradient = cast_half_precision(jnp.transpose(key_value[:, :, :head_width], (1, 0, 2)))
    value_gradient = cast_half_precision(jnp.transpose(key_value[:, :, head_width:], (1, 0, 2)))
    input_terms = (
        jnp.einsum("bqh,eh->bqe", query_gradient, w_query, preferred_element_type=jnp.float32)
        + jnp.einsum("bqh,eh->bqe", key_gradient, w_key, preferred_element_type=jnp.float32)
        + jnp.einsum("bqh,eh->bqe", value_gradient, w_value, preferred_element_type=jnp.float32)
    )
    grad_tokens = lax.psum_scatter(
        cast_half_precision(input_terms), "tp", scatter_dimension=2, tiled=True
    )
    reduced = lax.psum_scatter(
        half_concatenate(
            (
                jnp.einsum(
                    "bqe,bqh->eh", full_tokens, query_gradient, preferred_element_type=jnp.float32
                ),
                jnp.einsum(
                    "bqe,bqh->eh", full_tokens, key_gradient, preferred_element_type=jnp.float32
                ),
                jnp.einsum(
                    "bqe,bqh->eh", full_tokens, value_gradient, preferred_element_type=jnp.float32
                ),
                jnp.einsum(
                    "bqe,bqh->eh", full_grads, mixed_heads, preferred_element_type=jnp.float32
                ),
            ),
            axis=1,
        ),
        "ctx",
        scatter_dimension=0,
        tiled=True,
    )
    sum_query = reduced[:, :head_width]
    sum_key = reduced[:, head_width : 2 * head_width]
    sum_value = reduced[:, 2 * head_width : 3 * head_width]
    sum_out = reduced[:, 3 * head_width :]
    grad_query = cast_half_precision(sum_query)
    grad_key = cast_half_precision(sum_key)
    grad_value = cast_half_precision(sum_value)
    grad_out_proj = cast_half_precision(sum_out.T)
    return (attended, grad_tokens, grad_query, grad_key, grad_value, grad_out_proj)


def solution(mesh):
    placed = (
        P(None, "ctx", "tp"),
        P(None, "tp"),
        P(None, "tp"),
        P(None, "tp"),
        P("tp", None),
        P(None, "ctx", None),
        P(None, "ctx", "tp"),
    )
    return jax.shard_map(
        per_device,
        mesh=mesh,
        in_specs=placed,
        out_specs=(
            P(None, "ctx", "tp"),
            P(None, "ctx", "tp"),
            P("ctx", "tp"),
            P("ctx", "tp"),
            P("ctx", "tp"),
            P("tp", "ctx"),
        ),
        check_vma=False,
    )
```

```python
import functools

import jax
import jax.numpy as jnp
from jax import lax
from jax.experimental import pallas as pl
from jax.experimental.pallas import tpu as pltpu
from jax.sharding import PartitionSpec as P

HEAD_DIM = 128
FRAME = 16
MESH = pl.DeviceIdType.MESH
BF = jnp.bfloat16
F32 = jnp.float32

ORDER = ((2, 1), (1, 1), (3, 1), (1, 0), (3, 0), (2, 0), (0, 1), (0, 0))
INDEX = {offset: k for k, offset in enumerate(ORDER)}
GATHER_COPIES = 7
SCATTER_COPIES = 7


def dot(a, b):
    return jnp.dot(a, b, preferred_element_type=F32)


def dot_nt(a, b):
    return lax.dot_general(a, b, (((1,), (1,)), ((), ())), preferred_element_type=F32)


def dot_tn(a, b):
    return lax.dot_general(a, b, (((0,), (0,)), ((), ())), preferred_element_type=F32)


class Copies:
    def __init__(self, send_sems, recv_sems):
        self.send_sems, self.recv_sems = send_sems, recv_sems
        self.used = 0
        self.started = []

    def start(self, src, dst, device):
        k = self.used
        self.used += 1
        copy = pltpu.make_async_remote_copy(
            src_ref=src,
            dst_ref=dst,
            send_sem=self.send_sems.at[k],
            recv_sem=self.recv_sems.at[k],
            device_id=device,
            device_id_type=MESH,
        )
        copy.start()
        self.started.append(copy)
        return copy

    def finish(self):
        for copy in self.started:
            copy.wait_send()


class Gather:
    def __init__(self, copies, peer, own, slot, landing):
        self.copies, self.peer, self.slot, self.landing = copies, peer, slot, landing
        go = copies.start
        self.pair = go(own, landing(0, 1, 0, 0), peer(0, 1))
        self.far = go(own, landing(2, 0, 0, 0), peer(2, 0))
        self.up = go(own, landing(1, 0, 0, 0), peer(1, 0))
        self.down = go(own, landing(3, 0, 0, 0), peer(3, 0))

    def forward_pair(self):
        self.pair.wait_recv()
        go = self.copies.start
        self.up_pair = go(self.slot(0, 1), self.landing(1, 0, 0, 1), self.peer(1, 0))
        self.down_pair = go(self.slot(0, 1), self.landing(3, 0, 0, 1), self.peer(3, 0))

    def forward_far(self):
        self.far.wait_recv()
        self.far_pair = self.copies.start(
            self.slot(2, 0), self.landing(0, 1, 2, 0), self.peer(0, 1)
        )


class Scatter:
    def __init__(self, copies, peer, parts, landed, add):
        self.copies, self.peer, self.parts, self.landed, self.add = copies, peer, parts, landed, add

    def send(self, k):
        ring, pair = ORDER[k]
        to = self.peer(0, 1) if ring == 2 else self.peer(ring, 0)
        copy = self.copies.start(self.parts.at[k], self.landed.at[k], to)
        setattr(self, ("far_pair", "up_pair", "down_pair", "up", "down")[k], copy)

    def relay_far(self):
        self.far_pair.wait_recv()
        self.add(self.parts.at[5], (self.parts.at[5], self.landed.at[0]))
        self.far = self.copies.start(self.parts.at[5], self.landed.at[5], self.peer(2, 0))

    def relay_pair(self):
        self.up_pair.wait_recv()
        self.down_pair.wait_recv()
        self.add(
            self.parts.at[6], (self.parts.at[6], self.landed.at[1], self.landed.at[2])
        )
        self.pair = self.copies.start(self.parts.at[6], self.landed.at[6], self.peer(0, 1))

    def finish(self, store):
        for copy in (self.up, self.down, self.far, self.pair):
            copy.wait_recv()
        store(
            (
                self.parts.at[7],
                self.landed.at[3],
                self.landed.at[4],
                self.landed.at[5],
                self.landed.at[6],
            )
        )


def summed(refs, where):
    total = refs[0][where].astype(F32)
    for ref in refs[1:]:
        total = total + ref[where].astype(F32)
    return total


def add_rows(step):
    def add(dst, refs):
        def body(i, carry):
            where = (pl.ds(pl.multiple_of(i * step, step), step), slice(None))
            dst[where] = summed(refs, where).astype(dst.dtype)
            return carry

        lax.fori_loop(0, dst.shape[0] // step, body, 0)

    return add


def add_lead(dst, refs):
    def body(i, carry):
        dst[i] = summed(refs, i).astype(dst.dtype)
        return carry

    lax.fori_loop(0, dst.shape[0], body, 0)


def kernel(
    first_ref,
    tok_ref,
    wq_hbm,
    wk_hbm,
    wv_hbm,
    wo_hbm,
    gout_ref,
    att_out,
    dtok_out,
    gq_out,
    gk_out,
    gv_out,
    go_out,
    wq,
    wk,
    wv,
    wo,
    x_all,
    g_all,
    x_sib,
    g_sib,
    xt_all,
    qkv_acc,
    do_acc,
    q_own,
    do_own,
    kv,
    prob,
    mixed,
    mixed_sib,
    grads,
    grads_sib,
    kv_mate,
    kv_mate_in,
    att_parts,
    att_in,
    dkv_parts,
    dkv_in,
    dtok_parts,
    dtok_in,
    wo_parts,
    wo_in,
    wq_parts,
    wq_in,
    wkv_parts,
    wkv_in,
    send_sems,
    recv_sems,
    local_sems,
):
    ctx, tp = lax.axis_index("ctx"), lax.axis_index("tp")
    y, xh, core = ctx // 4, (ctx // 2) % 2, ctx % 2
    z, xl = tp // 2, tp % 2
    width = 512
    half = 256
    scale = HEAD_DIM ** (-0.5)

    def tp_peer(ring, pair):
        return (ctx, ((z + ring) % 4) * 2 + (xl + pair) % 2)

    def tp_at(ring, pair):
        return ((z + ring) % 4) * 2 + (xl + pair) % 2

    def ctx_peer(ring, pair):
        return (((y + ring) % 4) * 4 + ((xh + pair) % 2) * 2 + core, tp)

    def chip_at(ring, pair):
        return ((y + ring) % 4) * 2 + (xh + pair) % 2

    mate = (ctx + 1 - 2 * core, tp)

    local = [
        pltpu.make_async_copy(src, dst, local_sems.at[k])
        for k, (src, dst) in enumerate(
            (
                (tok_ref, x_all.at[tp]),
                (wq_hbm, wq),
                (wk_hbm, wk),
                (wv_hbm, wv),
                (wo_hbm, wo),
                (gout_ref, g_all.at[tp]),
            )
        )
    ]
    for copy in local:
        copy.start()

    barrier = pltpu.get_barrier_semaphore()
    neighbours = [
        at(ring, pair)
        for at in (tp_peer, ctx_peer)
        for ring, pair in ((0, 1), (1, 0), (2, 0), (3, 0))
    ] + [mate]
    for device in neighbours:
        pl.semaphore_signal(barrier, inc=1, device_id=device, device_id_type=MESH)
    pl.semaphore_wait(barrier, len(neighbours))

    copies = Copies(send_sems, recv_sems)

    def tp_gather(own, slots):
        return Gather(
            copies,
            tp_peer,
            own,
            lambda ring, pair: slots.at[tp_at(ring, pair)],
            lambda to_ring, to_pair, ring, pair: slots.at[tp_at(ring, pair)],
        )

    def ctx_landing(to_ring, to_pair, ring, pair):
        return kv.at[0, INDEX[((ring - to_ring) % 4, (pair + to_pair) % 2)]]

    tokens = tp_gather(tok_ref, x_all)

    def project(slot, first=False):
        x = x_all[slot]
        rows = pl.ds(pl.multiple_of(slot * width, width), width)
        for k, w in enumerate((wq, wk, wv)):
            term = dot(x, w[rows, :])
            where = (slice(None), slice(k * half, (k + 1) * half))
            if first:
                qkv_acc[where] = term
            else:
                qkv_acc[where] += term

    for copy in local[:4]:
        copy.wait()
    project(tp, first=True)
    tokens.forward_pair()
    project(tp_at(0, 1))
    tokens.forward_far()
    tokens.up.wait_recv()
    tokens.down.wait_recv()
    cotangents = tp_gather(gout_ref, g_all)
    project(tp_at(2, 0))
    project(tp_at(1, 0))
    project(tp_at(3, 0))
    tokens.up_pair.wait_recv()
    tokens.down_pair.wait_recv()
    project(tp_at(1, 1))
    project(tp_at(3, 1))
    tokens.far_pair.wait_recv()
    project(tp_at(2, 1))

    own_kv = kv.at[0, INDEX[(0, 0)]]
    for p in range(4):
        b, h = p // 2, p % 2
        rows = slice(b * 128, (b + 1) * 128)
        q_own[p] = qkv_acc[rows, h * 128 : (h + 1) * 128].astype(BF)
        own_kv[2 * p] = qkv_acc[rows, half + h * 128 : half + (h + 1) * 128].astype(BF)
        own_kv[2 * p + 1] = qkv_acc[
            rows, 2 * half + h * 128 : 2 * half + (h + 1) * 128
        ].astype(BF)

    rows_kv = Gather(
        copies, ctx_peer, own_kv, lambda ring, pair: kv.at[0, INDEX[(ring, pair)]], ctx_landing
    )
    shared = []

    def share(ring, pair):
        k = INDEX[(ring, pair)]
        shared.append(copies.start(kv.at[0, k], kv.at[1, k], mate))

    share(0, 0)
    other_half = pl.ds(pl.multiple_of((1 - core) * half, half), half)
    my_half = pl.ds(pl.multiple_of(core * half, half), half)
    x_half = copies.start(x_all.at[:, :, other_half], x_sib, mate)
    local[5].wait()
    cotangents.forward_pair()
    rows_kv.forward_pair()
    share(0, 1)
    cotangents.forward_far()
    x_half.wait_recv()

    def transpose_block(k, carry):
        xt_all[k, :, :half] = x_all[k, :, my_half].T
        xt_all[k, :, half:] = x_sib[k].T
        return carry

    lax.fori_loop(0, 8, transpose_block, 0)
    rows_kv.forward_far()
    share(2, 0)
    cotangents.up.wait_recv()
    cotangents.down.wait_recv()
    local[4].wait()

    def pull_back(slot, first=False):
        columns = pl.ds(pl.multiple_of(slot * width, width), width)
        term = dot_nt(g_all[slot], wo[:, columns])
        if first:
            do_acc[...] = term
        else:
            do_acc[...] += term

    pull_back(tp, first=True)
    for offset in ((0, 1), (2, 0), (1, 0), (3, 0)):
        pull_back(tp_at(*offset))
    rows_kv.up.wait_recv()
    share(3, 0)
    rows_kv.down.wait_recv()
    share(1, 0)
    cotangents.up_pair.wait_recv()
    cotangents.down_pair.wait_recv()
    pull_back(tp_at(1, 1))
    pull_back(tp_at(3, 1))
    cotangents.far_pair.wait_recv()
    pull_back(tp_at(2, 1))
    g_half = copies.start(g_all.at[:, :, other_half], g_sib, mate)
    for p in range(4):
        b, h = p // 2, p % 2
        do_own[p] = do_acc[b * 128 : (b + 1) * 128, h * 128 : (h + 1) * 128].astype(BF)
    rows_kv.up_pair.wait_recv()
    share(3, 1)
    rows_kv.down_pair.wait_recv()
    share(1, 1)
    rows_kv.far_pair.wait_recv()
    share(2, 1)
    for copy in shared:
        copy.wait_recv()

    key_frame = lax.broadcasted_iota(jnp.int32, (128, 128), 0) // FRAME
    frame_gap = key_frame - lax.broadcasted_iota(jnp.int32, (128, 128), 1) // FRAME
    frames = 128 // FRAME
    blocks = [
        [2 * chip_at(*ORDER[k]) + (core if d == 0 else 1 - core) for k in range(8)]
        for d in range(2)
    ]

    def forward(p, carry):
        b = p // 2
        q = q_own[p]
        lowest = first_ref[b]
        tops = []
        for d in range(2):
            keys = kv[d, :, 2 * p].reshape(8 * 128, HEAD_DIM)
            logits = (dot_nt(keys, q) * scale).reshape(8, 128, 128)
            for k in range(8):
                block = blocks[d][k]
                visible = (frame_gap <= (ctx - block) * frames) & (
                    key_frame >= (lowest - block) * frames
                )
                masked = jnp.where(visible, logits[k], -jnp.inf)
                prob[p, d, k] = masked
                tops.append(jnp.max(masked, axis=0, keepdims=True))
        top = functools.reduce(jnp.maximum, tops)
        total = jnp.zeros((1, 128), F32)
        for d in range(2):
            for k in range(8):
                exponent = jnp.exp(prob[p, d, k] - top)
                prob[p, d, k] = exponent
                total = total + jnp.sum(exponent, axis=0, keepdims=True)
        inverse = 1.0 / total
        out = jnp.zeros((128, HEAD_DIM), F32)
        for d in range(2):
            weights = prob[p, d] * inverse
            prob[p, d] = weights
            values = kv[d, :, 2 * p + 1].reshape(8 * 128, HEAD_DIM)
            out = out + dot_tn(weights.reshape(8 * 128, 128).astype(BF), values)
        rows = pl.ds(pl.multiple_of(b * 128, 128), 128)
        columns = pl.ds(pl.multiple_of((p % 2) * 128, 128), 128)
        mixed[rows, columns] = out.astype(BF)
        return carry

    lax.fori_loop(0, 4, forward, 0)

    mixed_copy = copies.start(mixed, mixed_sib, mate)
    attended = Scatter(copies, tp_peer, att_parts, att_in, add_rows(64))

    def out_part(k):
        columns = pl.ds(pl.multiple_of(tp_at(*ORDER[k]) * width, width), width)
        att_parts[k] = dot(mixed[...], wo[:, columns]).astype(BF)

    for k in range(8):
        out_part(k)
        if k < 5:
            attended.send(k)
    mixed_copy.wait_recv()
    g_half.wait_recv()

    out_grads = Scatter(copies, ctx_peer, wo_parts, wo_in, add_rows(64))
    for k in range(8):
        chip = chip_at(*ORDER[k])
        wo_parts[k] = (
            dot_tn(mixed[...], g_all[chip, :, my_half]) + dot_tn(mixed_sib[...], g_sib[chip])
        ).astype(BF)
        if k < 5:
            out_grads.send(k)

    def backward(d, out):
        def body(p, carry):
            rows = pl.ds(pl.multiple_of((p // 2) * 128, 128), 128)
            columns = pl.ds(pl.multiple_of((p % 2) * 128, 128), 128)
            q, do = q_own[p], do_own[p]
            inner = lax.dot_general(
                jnp.ones((8, HEAD_DIM), F32),
                do.astype(F32) * mixed[rows, columns].astype(F32),
                (((1,), (1,)), ((), ())),
                precision=lax.Precision.HIGHEST,
                preferred_element_type=F32,
            )[0:1]
            keys = kv[d, :, 2 * p].reshape(8 * 128, HEAD_DIM)
            values = kv[d, :, 2 * p + 1].reshape(8 * 128, HEAD_DIM)
            weights = prob[p, d].reshape(8 * 128, 128)
            slopes = (weights * (dot_nt(values, do) - inner) * scale).astype(BF)
            out[:, 2 * p] = dot(slopes, q).astype(BF).reshape(8, 128, HEAD_DIM)
            out[:, 2 * p + 1] = dot(weights.astype(BF), do).astype(BF).reshape(8, 128, HEAD_DIM)
            term = dot_tn(slopes, keys)
            if d == 1:
                do_acc[rows, columns] = term
            else:
                do_acc[rows, columns] += term
            return carry

        lax.fori_loop(0, 4, body, 0)

    backward(1, kv_mate)
    mate_copy = copies.start(kv_mate, kv_mate_in, mate)
    backward(0, dkv_parts)
    grads[:, :half] = do_acc[...].astype(BF)
    dq_copy = copies.start(grads.at[:, pl.ds(0, half)], grads_sib.at[:, pl.ds(0, half)], mate)
    mate_copy.wait_recv()
    kv_sums = Scatter(copies, ctx_peer, dkv_parts, dkv_in, add_lead)
    for k in range(8):
        add_lead(dkv_parts.at[k], (dkv_parts.at[k], kv_mate_in.at[k]))
        if k < 5:
            kv_sums.send(k)
    attended.relay_far()
    attended.relay_pair()
    out_grads.relay_far()
    out_grads.relay_pair()

    dq_copy.wait_recv()
    query_grads = Scatter(copies, ctx_peer, wq_parts, wq_in, add_rows(64))
    for k in range(8):
        chip = chip_at(*ORDER[k])
        wq_parts[k] = (
            dot(xt_all[chip, :, :half], grads[:, :half])
            + dot(xt_all[chip, :, half:], grads_sib[:, :half])
        ).astype(BF)
        if k < 5 and k != 0:
            query_grads.send(k)
    query_grads.send(0)
    kv_sums.relay_far()
    kv_sums.relay_pair()

    def store_rows(out):
        return lambda refs: add_rows(64)(out, refs)

    attended.finish(store_rows(att_out))
    out_grads.finish(store_rows(go_out))

    def store_kv(refs):
        for p in range(4):
            b, h = p // 2, p % 2
            for which in range(2):
                at = (1 + which) * half + h * 128
                grads[b * 128 : (b + 1) * 128, at : at + 128] = summed(
                    refs, 2 * p + which
                ).astype(BF)

    kv_sums.finish(store_kv)
    kv_columns = pl.ds(half, 2 * half)
    dkv_copy = copies.start(grads.at[:, kv_columns], grads_sib.at[:, kv_columns], mate)

    token_grads = Scatter(copies, tp_peer, dtok_parts, dtok_in, add_rows(64))
    for k in range(8):
        rows = pl.ds(pl.multiple_of(tp_at(*ORDER[k]) * width, width), width)
        dtok_parts[k] = (
            dot_nt(grads[:, :half], wq[rows, :])
            + dot_nt(grads[:, half : 2 * half], wk[rows, :])
            + dot_nt(grads[:, 2 * half :], wv[rows, :])
        ).astype(BF)
        if k < 5:
            token_grads.send(k)

    dkv_copy.wait_recv()
    kv_grads = Scatter(copies, ctx_peer, wkv_parts, wkv_in, add_rows(64))
    for k in range(8):
        chip = chip_at(*ORDER[k])
        wkv_parts[k] = (
            dot(xt_all[chip, :, :half], grads[:, half:])
            + dot(xt_all[chip, :, half:], grads_sib[:, half:])
        ).astype(BF)
        if k < 5:
            kv_grads.send(k)
    query_grads.relay_far()
    query_grads.relay_pair()
    token_grads.relay_far()
    token_grads.relay_pair()
    kv_grads.relay_far()
    kv_grads.relay_pair()
    query_grads.finish(store_rows(gq_out))
    token_grads.finish(store_rows(dtok_out))

    def store_pair(refs):
        def body(i, carry):
            rows = pl.ds(pl.multiple_of(i * 64, 64), 64)
            total = summed(refs, (rows, slice(None))).astype(BF)
            gk_out[rows, :] = total[:, :half]
            gv_out[rows, :] = total[:, half:]
            return carry

        lax.fori_loop(0, 4, body, 0)

    kv_grads.finish(store_pair)
    copies.finish()


N_COPIES = 3 * GATHER_COPIES + 6 * SCATTER_COPIES + 8 + 6


def per_device(tokens, w_query, w_key, w_value, w_out, allowed, grad_out):
    batch, block, width = tokens.shape
    rows = batch * block
    head_width = w_query.shape[1]
    first = lax.axis_index("ctx") + 1 - jnp.sum(allowed[:, 0, :], axis=1, dtype=jnp.int32)
    vmem = pl.BlockSpec(memory_space=pltpu.VMEM)
    hbm = pl.BlockSpec(memory_space=pl.ANY)

    def halves(*shape):
        return pltpu.VMEM(shape, BF)

    def pair(*shape):
        return [halves(8, *shape), halves(7, *shape)]

    outs = pl.pallas_call(
        kernel,
        out_shape=[jax.ShapeDtypeStruct((rows, width), BF)] * 2
        + [jax.ShapeDtypeStruct((head_width, head_width), BF)] * 4,
        in_specs=[pl.BlockSpec(memory_space=pltpu.SMEM)] + [hbm] * 6,
        out_specs=[vmem] * 6,
        scratch_shapes=[
            halves(4096, 256),
            halves(4096, 256),
            halves(4096, 256),
            halves(256, 4096),
            halves(8, 256, 512),
            halves(8, 256, 512),
            halves(8, 256, 256),
            halves(8, 256, 256),
            halves(8, 256, 512),
            pltpu.VMEM((256, 768), F32),
            pltpu.VMEM((256, 256), F32),
            halves(4, 128, 128),
            halves(4, 128, 128),
            halves(2, 8, 8, 128, 128),
            pltpu.VMEM((4, 2, 8, 128, 128), F32),
            halves(256, 256),
            halves(256, 256),
            halves(256, 768),
            halves(256, 768),
            halves(8, 8, 128, 128),
            halves(8, 8, 128, 128),
            *pair(256, 512),
            *pair(8, 128, 128),
            *pair(256, 512),
            *pair(256, 256),
            *pair(256, 256),
            *pair(256, 512),
            pltpu.SemaphoreType.DMA((N_COPIES,)),
            pltpu.SemaphoreType.DMA((N_COPIES,)),
            pltpu.SemaphoreType.DMA((6,)),
        ],
        compiler_params=pltpu.CompilerParams(
            collective_id=0, has_side_effects=True, vmem_limit_bytes=60 * 2**20
        ),
    )(
        first,
        tokens.reshape(rows, width),
        w_query,
        w_key,
        w_value,
        w_out,
        grad_out.reshape(rows, width),
    )
    attended, grad_tokens, *weight_grads = outs
    return (
        attended.reshape(batch, block, width),
        grad_tokens.reshape(batch, block, width),
        *weight_grads,
    )


def solution(mesh):
    placed = (
        P(None, "ctx", "tp"),
        P(None, "tp"),
        P(None, "tp"),
        P(None, "tp"),
        P("tp", None),
        P(None, "ctx", None),
        P(None, "ctx", "tp"),
    )
    return jax.shard_map(
        per_device,
        mesh=mesh,
        in_specs=placed,
        out_specs=(
            P(None, "ctx", "tp"),
            P(None, "ctx", "tp"),
            P("ctx", "tp"),
            P("ctx", "tp"),
            P("ctx", "tp"),
            P("tp", "ctx"),
        ),
        check_vma=False,
    )
```

```python
import functools

import jax
import jax.numpy as jnp
from jax import lax
from jax.experimental import pallas as pl
from jax.experimental.pallas import tpu as pltpu
from jax.sharding import PartitionSpec as P

HEAD_DIM = 128
FRAME = 16
MESH = pl.DeviceIdType.MESH
BF = jnp.bfloat16
F32 = jnp.float32

ORDER = ((2, 1), (1, 1), (3, 1), (1, 0), (3, 0), (2, 0), (0, 1), (0, 0))
INDEX = {offset: k for k, offset in enumerate(ORDER)}
GATHER_COPIES = 7
SCATTER_COPIES = 7


def dot(a, b):
    return jnp.dot(a, b, preferred_element_type=F32)


def dot_nt(a, b):
    return lax.dot_general(a, b, (((1,), (1,)), ((), ())), preferred_element_type=F32)


def dot_tn(a, b):
    return lax.dot_general(a, b, (((0,), (0,)), ((), ())), preferred_element_type=F32)


class Copies:
    def __init__(self, send_sems, recv_sems):
        self.send_sems, self.recv_sems = send_sems, recv_sems
        self.used = 0
        self.started = []

    def start(self, src, dst, device):
        k = self.used
        self.used += 1
        copy = pltpu.make_async_remote_copy(
            src_ref=src,
            dst_ref=dst,
            send_sem=self.send_sems.at[k],
            recv_sem=self.recv_sems.at[k],
            device_id=device,
            device_id_type=MESH,
        )
        copy.start()
        self.started.append(copy)
        return copy

    def finish(self):
        for copy in self.started:
            copy.wait_send()


class Gather:
    def __init__(self, copies, peer, own, slot, landing):
        self.copies, self.peer, self.slot, self.landing = copies, peer, slot, landing
        go = copies.start
        self.pair = go(own, landing(0, 1, 0, 0), peer(0, 1))
        self.far = go(own, landing(2, 0, 0, 0), peer(2, 0))
        self.up = go(own, landing(1, 0, 0, 0), peer(1, 0))
        self.down = go(own, landing(3, 0, 0, 0), peer(3, 0))

    def forward_pair(self):
        self.pair.wait_recv()
        go = self.copies.start
        self.up_pair = go(self.slot(0, 1), self.landing(1, 0, 0, 1), self.peer(1, 0))
        self.down_pair = go(self.slot(0, 1), self.landing(3, 0, 0, 1), self.peer(3, 0))

    def forward_far(self):
        self.far.wait_recv()
        self.far_pair = self.copies.start(
            self.slot(2, 0), self.landing(0, 1, 2, 0), self.peer(0, 1)
        )


class Scatter:
    def __init__(self, copies, peer, parts, landed, add):
        self.copies, self.peer, self.parts, self.landed, self.add = copies, peer, parts, landed, add

    def send(self, k):
        ring, pair = ORDER[k]
        to = self.peer(0, 1) if ring == 2 else self.peer(ring, 0)
        copy = self.copies.start(self.parts.at[k], self.landed.at[k], to)
        setattr(self, ("far_pair", "up_pair", "down_pair", "up", "down")[k], copy)

    def relay_far(self):
        self.far_pair.wait_recv()
        self.add(self.parts.at[5], (self.parts.at[5], self.landed.at[0]))
        self.far = self.copies.start(self.parts.at[5], self.landed.at[5], self.peer(2, 0))

    def relay_pair(self):
        self.up_pair.wait_recv()
        self.down_pair.wait_recv()
        self.add(
            self.parts.at[6], (self.parts.at[6], self.landed.at[1], self.landed.at[2])
        )
        self.pair = self.copies.start(self.parts.at[6], self.landed.at[6], self.peer(0, 1))

    def finish(self, store):
        for copy in (self.up, self.down, self.far, self.pair):
            copy.wait_recv()
        store(
            (
                self.parts.at[7],
                self.landed.at[3],
                self.landed.at[4],
                self.landed.at[5],
                self.landed.at[6],
            )
        )


def summed(refs, where):
    total = refs[0][where].astype(F32)
    for ref in refs[1:]:
        total = total + ref[where].astype(F32)
    return total


def add_rows(step):
    def add(dst, refs):
        def body(i, carry):
            where = (pl.ds(pl.multiple_of(i * step, step), step), slice(None))
            dst[where] = summed(refs, where).astype(dst.dtype)
            return carry

        lax.fori_loop(0, dst.shape[0] // step, body, 0)

    return add


def kernel(
    allowed_ref,
    tok_ref,
    wq_hbm,
    wk_hbm,
    wv_hbm,
    wo_hbm,
    gout_ref,
    att_out,
    dtok_out,
    gq_out,
    gk_out,
    gv_out,
    go_out,
    wq,
    wk,
    wv,
    wo,
    x_all,
    g_all,
    x_sib,
    g_sib,
    xt_all,
    qkv_acc,
    do_acc,
    low,
    pieces,
    cot_pieces,
    kv,
    cots,
    prob,
    mix_acc,
    mix_here,
    mix_in,
    dq_here,
    dq_in,
    mixed,
    mixed_sib,
    grads,
    grads_sib,
    kv_mate,
    kv_mate_in,
    dkv_parts,
    dkv_in,
    att_parts,
    att_in,
    dtok_parts,
    dtok_in,
    wo_parts,
    wo_in,
    wq_parts,
    wq_in,
    wkv_parts,
    wkv_in,
    send_sems,
    recv_sems,
    local_sems,
):
    ctx, tp = lax.axis_index("ctx"), lax.axis_index("tp")
    y, xh, core = ctx // 4, (ctx // 2) % 2, ctx % 2
    z, xl = tp // 2, tp % 2
    width = 512
    half = 256
    scale = HEAD_DIM ** (-0.5)

    def tp_peer(ring, pair):
        return (ctx, ((z + ring) % 4) * 2 + (xl + pair) % 2)

    def tp_at(ring, pair):
        return ((z + ring) % 4) * 2 + (xl + pair) % 2

    def ctx_peer(ring, pair):
        return (((y + ring) % 4) * 4 + ((xh + pair) % 2) * 2 + core, tp)

    def chip_at(ring, pair):
        return ((y + ring) % 4) * 2 + (xh + pair) % 2

    mate = (ctx + 1 - 2 * core, tp)

    local = [
        pltpu.make_async_copy(src, dst, local_sems.at[k])
        for k, (src, dst) in enumerate(
            (
                (tok_ref, x_all.at[tp]),
                (wq_hbm, wq),
                (wk_hbm, wk),
                (wv_hbm, wv),
                (wo_hbm, wo),
                (gout_ref, g_all.at[tp]),
            )
        )
    ]
    for copy in local:
        copy.start()

    barrier = pltpu.get_barrier_semaphore()
    neighbours = [tp_peer(ring, pair) for ring, pair in ((0, 1), (1, 0), (2, 0), (3, 0))]
    neighbours += [ctx_peer(*offset) for offset in ORDER[:7]] + [mate]
    for device in neighbours:
        pl.semaphore_signal(barrier, inc=1, device_id=device, device_id_type=MESH)
    pl.semaphore_wait(barrier, len(neighbours))

    copies = Copies(send_sems, recv_sems)

    def tp_gather(own, slots):
        return Gather(
            copies,
            tp_peer,
            own,
            lambda ring, pair: slots.at[tp_at(ring, pair)],
            lambda to_ring, to_pair, ring, pair: slots.at[tp_at(ring, pair)],
        )

    def turn(ring):
        return (y + ring) % 4

    def exchange(source, target):
        return [
            copies.start(source(turn(ring)), target, ctx_peer(ring, 0)) for ring in (1, 2, 3)
        ]

    def arrived(started):
        for copy in started:
            copy.wait_recv()

    for b in range(2):
        seen = allowed_ref[b, 0]
        for k in range(1, 16):
            seen = seen + allowed_ref[b, k]
        start = (ctx + 1 - seen) * (128 // FRAME)
        low[y, b] = jnp.full((8, 128), start.astype(F32))

    tokens = tp_gather(tok_ref, x_all)
    lows = exchange(lambda to: low.at[y], low.at[y])

    def project(slot, first=False):
        x = x_all[slot]
        rows = pl.ds(pl.multiple_of(slot * width, width), width)
        for k, w in enumerate((wq, wk, wv)):
            term = dot(x, w[rows, :])
            where = (slice(None), slice(k * half, (k + 1) * half))
            if first:
                qkv_acc[where] = term
            else:
                qkv_acc[where] += term

    for copy in local[:4]:
        copy.wait()
    project(tp, first=True)
    tokens.forward_pair()
    project(tp_at(0, 1))
    tokens.forward_far()
    tokens.up.wait_recv()
    tokens.down.wait_recv()
    cotangents = tp_gather(gout_ref, g_all)
    project(tp_at(2, 0))
    project(tp_at(1, 0))
    project(tp_at(3, 0))
    tokens.up_pair.wait_recv()
    tokens.down_pair.wait_recv()
    project(tp_at(1, 1))
    project(tp_at(3, 1))
    tokens.far_pair.wait_recv()
    project(tp_at(2, 1))

    for p in range(4):
        b, h = p // 2, p % 2
        rows = slice(b * 128, (b + 1) * 128)
        for place, which in enumerate((1, 2, 0)):
            at = which * half + h * 128
            pieces[p, place] = qkv_acc[rows, at : at + 128].astype(BF)

    from_side = [
        copies.start(pieces.at[turn(ring), pl.ds(0, 2)], kv.at[y, 0, 1, pl.ds(0, 2)], ctx_peer(ring, 1))
        for ring in range(4)
    ]
    from_rows = exchange(lambda to: pieces.at[to], kv.at[y, 0, 0])
    kv[y, 0, 0] = pieces[y]

    def share(side):
        return copies.start(
            kv.at[:, 0, side, pl.ds(0, 2)], kv.at[:, 1, side, pl.ds(0, 2)], mate
        )

    other_half = pl.ds(pl.multiple_of((1 - core) * half, half), half)
    my_half = pl.ds(pl.multiple_of(core * half, half), half)
    x_half = copies.start(x_all.at[:, :, other_half], x_sib, mate)
    local[5].wait()
    cotangents.forward_pair()
    x_half.wait_recv()

    def transpose_block(k, carry):
        xt_all[k, :, :half] = x_all[k, :, my_half].T
        xt_all[k, :, half:] = x_sib[k].T
        return carry

    lax.fori_loop(0, 8, transpose_block, 0)
    arrived(from_rows)
    shared = [share(0)]
    arrived(from_side)
    shared.append(share(1))
    cotangents.forward_far()
    arrived(shared)
    arrived(lows)

    key_frame = lax.broadcasted_iota(jnp.int32, (128, 128), 0) // FRAME
    frame_gap = key_frame - lax.broadcasted_iota(jnp.int32, (128, 128), 1) // FRAME
    frames = 128 // FRAME
    sides = [(d, side) for d in range(2) for side in range(2)]
    place_of = {
        (d, side): 2 * ((xh + side) % 2) + (core if d == 0 else 1 - core) for d, side in sides
    }
    queries = kv[:, 0, 0, 2].reshape(512, HEAD_DIM)
    batch_here = y // 2
    lowest = jnp.concatenate([low[k, batch_here][0:1] for k in range(4)], axis=1)
    tops = [[] for _ in range(4)]
    for ys in range(4):
        for n, (d, side) in enumerate(sides):
            rows = slice(n * 128, (n + 1) * 128)
            logits = dot_nt(kv[ys, d, side, 0], queries[ys * 128 :]) * scale
            place = place_of[d, side]
            begin = ((4 * ys + place) * frames).astype(F32)
            logits = logits + jnp.where(lowest[:, ys * 128 :] <= begin, 0.0, -jnp.inf)
            ahead = (place_of[0, 0] - place) * frames
            for k in range(ys, 4):
                part = logits[:, (k - ys) * 128 : (k - ys + 1) * 128]
                if k == ys:
                    part = jnp.where(frame_gap <= ahead, part, -jnp.inf)
                prob[ys, rows, k * 128 : (k + 1) * 128] = part
                tops[k].append(jnp.max(part, axis=0, keepdims=True))
    top = jnp.concatenate([functools.reduce(jnp.maximum, t) for t in tops], axis=1)
    totals = [jnp.zeros((1, 128), F32)] * 4
    for ys in range(4):
        for n in range(4):
            rows = slice(n * 128, (n + 1) * 128)
            exponent = jnp.exp(prob[ys, rows, ys * 128 :] - top[:, ys * 128 :])
            prob[ys, rows, ys * 128 :] = exponent
            sums = jnp.sum(exponent, axis=0, keepdims=True)
            for k in range(ys, 4):
                totals[k] = totals[k] + sums[:, (k - ys) * 128 : (k - ys + 1) * 128]
    inverse = 1.0 / jnp.concatenate(totals, axis=1)
    for ys in range(4):
        weights = prob[ys, :, ys * 128 :] * inverse[:, ys * 128 :]
        prob[ys, :, ys * 128 :] = weights
        values = kv[ys, :, :, 1].reshape(512, HEAD_DIM)
        term = dot_tn(weights.astype(BF), values)
        if ys == 0:
            mix_acc[...] = term
        else:
            mix_acc[ys * 128 :] += term
    mix_here[...] = mix_acc[...].astype(BF).reshape(4, 128, HEAD_DIM)
    from_mix = exchange(lambda to: mix_here.at[to], mix_in.at[y])
    mix_in[y] = mix_here[y]
    cotangents.up.wait_recv()
    cotangents.down.wait_recv()
    local[4].wait()

    def pull_back(slot, first=False):
        columns = pl.ds(pl.multiple_of(slot * width, width), width)
        term = dot_nt(g_all[slot], wo[:, columns])
        if first:
            do_acc[...] = term
        else:
            do_acc[...] += term

    pull_back(tp, first=True)
    for offset in ((0, 1), (2, 0), (1, 0), (3, 0)):
        pull_back(tp_at(*offset))
    cotangents.up_pair.wait_recv()
    cotangents.down_pair.wait_recv()
    pull_back(tp_at(1, 1))
    pull_back(tp_at(3, 1))
    cotangents.far_pair.wait_recv()
    pull_back(tp_at(2, 1))
    g_half = copies.start(g_all.at[:, :, other_half], g_sib, mate)
    for p in range(4):
        b, h = p // 2, p % 2
        cot_pieces[p] = do_acc[b * 128 : (b + 1) * 128, h * 128 : (h + 1) * 128].astype(BF)
    from_cots = exchange(lambda to: cot_pieces.at[to], cots.at[y])
    cots[y] = cot_pieces[y]

    def assemble(target, arrivals):
        for p in range(4):
            b, h = p // 2, p % 2
            target[b * 128 : (b + 1) * 128, h * 128 : (h + 1) * 128] = arrivals[p]

    arrived(from_mix)
    assemble(mixed, mix_in)

    mixed_copy = copies.start(mixed, mixed_sib, mate)
    attended = Scatter(copies, tp_peer, att_parts, att_in, add_rows(64))

    def out_part(k):
        columns = pl.ds(pl.multiple_of(tp_at(*ORDER[k]) * width, width), width)
        att_parts[k] = dot(mixed[...], wo[:, columns]).astype(BF)

    for k in range(8):
        out_part(k)
        if k < 5:
            attended.send(k)
    mixed_copy.wait_recv()
    g_half.wait_recv()

    out_grads = Scatter(copies, ctx_peer, wo_parts, wo_in, add_rows(64))
    for k in range(8):
        chip = chip_at(*ORDER[k])
        wo_parts[k] = (
            dot_tn(mixed[...], g_all[chip, :, my_half]) + dot_tn(mixed_sib[...], g_sib[chip])
        ).astype(BF)
        if k < 5:
            out_grads.send(k)

    arrived(from_cots)
    cot_rows = cots[...].reshape(512, HEAD_DIM)
    inner = lax.dot_general(
        jnp.ones((8, HEAD_DIM), F32),
        cot_rows.astype(F32) * mix_here[...].reshape(512, HEAD_DIM).astype(F32),
        (((1,), (1,)), ((), ())),
        precision=lax.Precision.HIGHEST,
        preferred_element_type=F32,
    )[0:1]
    mate_copies = []
    for ys in range(4):
        keys = kv[ys, :, :, 0].reshape(512, HEAD_DIM)
        values = kv[ys, :, :, 1].reshape(512, HEAD_DIM)
        weights = prob[ys, :, ys * 128 :]
        slopes = (
            weights * (dot_nt(values, cot_rows[ys * 128 :]) - inner[:, ys * 128 :]) * scale
        ).astype(BF)
        key_part = dot(slopes, queries[ys * 128 :]).astype(BF).reshape(2, 2, 128, HEAD_DIM)
        value_part = (
            dot(weights.astype(BF), cot_rows[ys * 128 :]).astype(BF).reshape(2, 2, 128, HEAD_DIM)
        )
        dkv_parts[ys, :, 0] = key_part[0]
        dkv_parts[ys, :, 1] = value_part[0]
        kv_mate[ys, :, 0] = key_part[1]
        kv_mate[ys, :, 1] = value_part[1]
        mate_copies.append(copies.start(kv_mate.at[ys], kv_mate_in.at[ys], mate))
        term = dot_tn(slopes, keys)
        if ys == 0:
            mix_acc[...] = term
        else:
            mix_acc[ys * 128 :] += term
    dq_here[...] = mix_acc[...].astype(BF).reshape(4, 128, HEAD_DIM)
    from_dq = exchange(lambda to: dq_here.at[to], dq_in.at[y])
    dq_in[y] = dq_here[y]
    for ys in range(4):
        mate_copies[ys].wait_recv()
        for side in range(2):
            dkv_parts[ys, side] = summed((dkv_parts, kv_mate_in), (ys, side)).astype(BF)
    from_dkv = [
        copies.start(dkv_parts.at[turn(ring), side], dkv_in.at[y, side], ctx_peer(ring, side))
        for ring in (2, 1, 3, 0)
        for side in (1, 0)
        if (ring, side) != (0, 0)
    ]
    dkv_in[y, 0] = dkv_parts[y, 0]
    arrived(from_dq)
    assemble(grads, dq_in)
    dq_copy = copies.start(grads.at[:, pl.ds(0, half)], grads_sib.at[:, pl.ds(0, half)], mate)
    attended.relay_far()
    attended.relay_pair()
    out_grads.relay_far()
    out_grads.relay_pair()

    dq_copy.wait_recv()
    query_grads = Scatter(copies, ctx_peer, wq_parts, wq_in, add_rows(64))
    for k in range(8):
        chip = chip_at(*ORDER[k])
        wq_parts[k] = (
            dot(xt_all[chip, :, :half], grads[:, :half])
            + dot(xt_all[chip, :, half:], grads_sib[:, :half])
        ).astype(BF)
        if k < 5 and k != 0:
            query_grads.send(k)
    query_grads.send(0)

    def store_rows(out):
        return lambda refs: add_rows(64)(out, refs)

    attended.finish(store_rows(att_out))
    out_grads.finish(store_rows(go_out))

    arrived(from_dkv)
    for p in range(4):
        b, h = p // 2, p % 2
        for which in range(2):
            at = (1 + which) * half + h * 128
            grads[b * 128 : (b + 1) * 128, at : at + 128] = summed(
                (dkv_in.at[:, 0], dkv_in.at[:, 1]), (p, which)
            ).astype(BF)
    kv_columns = pl.ds(half, 2 * half)
    dkv_copy = copies.start(grads.at[:, kv_columns], grads_sib.at[:, kv_columns], mate)

    token_grads = Scatter(copies, tp_peer, dtok_parts, dtok_in, add_rows(64))
    for k in range(8):
        rows = pl.ds(pl.multiple_of(tp_at(*ORDER[k]) * width, width), width)
        dtok_parts[k] = (
            dot_nt(grads[:, :half], wq[rows, :])
            + dot_nt(grads[:, half : 2 * half], wk[rows, :])
            + dot_nt(grads[:, 2 * half :], wv[rows, :])
        ).astype(BF)
        if k < 5:
            token_grads.send(k)

    dkv_copy.wait_recv()
    kv_grads = Scatter(copies, ctx_peer, wkv_parts, wkv_in, add_rows(64))
    for k in range(8):
        chip = chip_at(*ORDER[k])
        wkv_parts[k] = (
            dot(xt_all[chip, :, :half], grads[:, half:])
            + dot(xt_all[chip, :, half:], grads_sib[:, half:])
        ).astype(BF)
        if k < 5:
            kv_grads.send(k)
    query_grads.relay_far()
    query_grads.relay_pair()
    token_grads.relay_far()
    token_grads.relay_pair()
    kv_grads.relay_far()
    kv_grads.relay_pair()
    query_grads.finish(store_rows(gq_out))
    token_grads.finish(store_rows(dtok_out))

    def store_pair(refs):
        def body(i, carry):
            rows = pl.ds(pl.multiple_of(i * 64, 64), 64)
            total = summed(refs, (rows, slice(None))).astype(BF)
            gk_out[rows, :] = total[:, :half]
            gv_out[rows, :] = total[:, half:]
            return carry

        lax.fori_loop(0, 4, body, 0)

    kv_grads.finish(store_pair)
    copies.finish()


def settle(*refs):
    sources, results, held, sems = refs[:6], refs[6:12], refs[12:18], refs[18]
    reads = [pltpu.make_async_copy(sources[k], held[k], sems.at[k]) for k in range(6)]
    writes = [pltpu.make_async_copy(held[k], results[k], sems.at[6 + k]) for k in range(6)]
    for read in reads:
        read.start()
    for read, write in zip(reads, writes):
        read.wait()
        write.start()
    for write in writes:
        write.wait()


N_COPIES = 2 * GATHER_COPIES + 5 * SCATTER_COPIES + 26 + 2 + 4 + 5


def per_device(tokens, w_query, w_key, w_value, w_out, allowed, grad_out):
    batch, block, width = tokens.shape
    rows = batch * block
    head_width = w_query.shape[1]
    vmem = pl.BlockSpec(memory_space=pltpu.VMEM)
    hbm = pl.BlockSpec(memory_space=pl.ANY)

    def halves(*shape):
        return pltpu.VMEM(shape, BF)

    def pair(*shape):
        return [halves(8, *shape), halves(7, *shape)]

    outs = pl.pallas_call(
        kernel,
        out_shape=[jax.ShapeDtypeStruct((rows, width), BF)] * 2
        + [jax.ShapeDtypeStruct((head_width, head_width), BF)] * 4,
        in_specs=[pl.BlockSpec(memory_space=pltpu.SMEM)] + [hbm] * 6,
        out_specs=[vmem] * 6,
        scratch_shapes=[
            halves(4096, 256),
            halves(4096, 256),
            halves(4096, 256),
            halves(256, 4096),
            halves(8, 256, 512),
            halves(8, 256, 512),
            halves(8, 256, 256),
            halves(8, 256, 256),
            halves(8, 256, 512),
            pltpu.VMEM((256, 768), F32),
            pltpu.VMEM((256, 256), F32),
            pltpu.VMEM((4, 2, 8, 128), F32),
            halves(4, 3, 128, 128),
            halves(4, 128, 128),
            halves(4, 2, 2, 3, 128, 128),
            halves(4, 128, 128),
            pltpu.VMEM((4, 512, 512), F32),
            pltpu.VMEM((512, 128), F32),
            halves(4, 128, 128),
            halves(4, 128, 128),
            halves(4, 128, 128),
            halves(4, 128, 128),
            halves(256, 256),
            halves(256, 256),
            halves(256, 768),
            halves(256, 768),
            halves(4, 2, 2, 128, 128),
            halves(4, 2, 2, 128, 128),
            halves(4, 2, 2, 128, 128),
            halves(4, 2, 2, 128, 128),
            *pair(256, 512),
            *pair(256, 512),
            *pair(256, 256),
            *pair(256, 256),
            *pair(256, 512),
            pltpu.SemaphoreType.DMA((N_COPIES,)),
            pltpu.SemaphoreType.DMA((N_COPIES,)),
            pltpu.SemaphoreType.DMA((6,)),
        ],
        compiler_params=pltpu.CompilerParams(
            collective_id=0, has_side_effects=True, vmem_limit_bytes=60 * 2**20
        ),
    )(
        allowed.reshape(batch, allowed.shape[2]),
        tokens.reshape(rows, width),
        w_query,
        w_key,
        w_value,
        w_out,
        grad_out.reshape(rows, width),
    )
    attended, grad_tokens, *weight_grads = pl.pallas_call(
        settle,
        out_shape=[jax.ShapeDtypeStruct(out.shape, out.dtype) for out in outs],
        in_specs=[hbm] * 6,
        out_specs=[hbm] * 6,
        scratch_shapes=[pltpu.VMEM(out.shape, out.dtype) for out in outs]
        + [pltpu.SemaphoreType.DMA((12,))],
    )(*outs)
    return (
        attended.reshape(batch, block, width),
        grad_tokens.reshape(batch, block, width),
        *weight_grads,
    )


def solution(mesh):
    placed = (
        P(None, "ctx", "tp"),
        P(None, "tp"),
        P(None, "tp"),
        P(None, "tp"),
        P("tp", None),
        P(None, "ctx", None),
        P(None, "ctx", "tp"),
    )
    return jax.shard_map(
        per_device,
        mesh=mesh,
        in_specs=placed,
        out_specs=(
            P(None, "ctx", "tp"),
            P(None, "ctx", "tp"),
            P("ctx", "tp"),
            P("ctx", "tp"),
            P("ctx", "tp"),
            P("tp", "ctx"),
        ),
        check_vma=False,
    )
```

```python
import functools

import jax
import jax.numpy as jnp
from jax import lax
from jax.experimental import pallas as pl
from jax.experimental.pallas import tpu as pltpu
from jax.sharding import PartitionSpec as P

HEAD_DIM = 128
FRAME = 16
MESH = pl.DeviceIdType.MESH
BF = jnp.bfloat16
F32 = jnp.float32

ORDER = ((2, 1), (1, 1), (3, 1), (2, 0), (1, 0), (3, 0), (0, 1), (0, 0))
GATHER_COPIES = 7
SCATTER_COPIES = 13


def dot(a, b):
    return jnp.dot(a, b, preferred_element_type=F32)


def dot_nt(a, b):
    return lax.dot_general(a, b, (((1,), (1,)), ((), ())), preferred_element_type=F32)


def dot_tn(a, b):
    return lax.dot_general(a, b, (((0,), (0,)), ((), ())), preferred_element_type=F32)


class Copies:
    def __init__(self, send_sems, recv_sems):
        self.send_sems, self.recv_sems = send_sems, recv_sems
        self.used = 0
        self.started = []

    def start(self, src, dst, device):
        k = self.used
        self.used += 1
        copy = pltpu.make_async_remote_copy(
            src_ref=src,
            dst_ref=dst,
            send_sem=self.send_sems.at[k],
            recv_sem=self.recv_sems.at[k],
            device_id=device,
            device_id_type=MESH,
        )
        copy.start()
        self.started.append(copy)
        return copy

    def finish(self):
        for copy in self.started:
            copy.wait_send()


class Gather:
    def __init__(self, copies, peer, own, slot, landing):
        self.copies, self.peer, self.slot, self.landing = copies, peer, slot, landing
        go = copies.start
        self.pair = go(own, landing(0, 1, 0, 0), peer(0, 1))
        self.far = go(own, landing(2, 0, 0, 0), peer(2, 0))
        self.up = go(own, landing(1, 0, 0, 0), peer(1, 0))
        self.down = go(own, landing(3, 0, 0, 0), peer(3, 0))

    def forward_pair(self):
        self.pair.wait_recv()
        go = self.copies.start
        self.up_pair = go(self.slot(0, 1), self.landing(1, 0, 0, 1), self.peer(1, 0))
        self.down_pair = go(self.slot(0, 1), self.landing(3, 0, 0, 1), self.peer(3, 0))

    def forward_far(self):
        self.far.wait_recv()
        self.far_pair = self.copies.start(
            self.slot(2, 0), self.landing(0, 1, 2, 0), self.peer(0, 1)
        )


class Scatter:
    def __init__(self, copies, peer, parts, landed, add):
        self.copies, self.peer, self.parts, self.landed, self.add = copies, peer, parts, landed, add
        rows = parts.shape[1] // 2
        self.low, self.high = pl.ds(0, rows), pl.ds(rows, rows)
        self.far, self.near = [[], []], [[], []]

    def move(self, k, slot, rows, ring):
        return self.copies.start(
            self.parts.at[k, rows], self.landed.at[slot, rows], self.peer(ring, 0)
        )

    def send(self, k):
        if k >= 6:
            return
        ring, pair = ORDER[k]
        slot = 3 * pair
        if ring == 2:
            self.far[pair] = [self.move(k, slot, self.low, 1), self.move(k, slot, self.high, 3)]
        elif ring == 1:
            self.near[pair].append(self.move(k, slot + 1, self.high, 1))
        else:
            self.near[pair].append(self.move(k, slot + 2, self.low, 3))

    def relay(self):
        for pair in (1, 0):
            first, slot = 3 - 3 * pair, 3 * pair
            for copy, k, to, rows, ring in (
                (self.far[pair][0], first + 1, slot + 1, self.low, 1),
                (self.far[pair][1], first + 2, slot + 2, self.high, 3),
            ):
                copy.wait_recv()
                part = self.parts.at[k, rows]
                self.add(part, (part, self.landed.at[slot, rows]))
                self.near[pair].append(self.move(k, to, rows, ring))

    def cross(self):
        for copy in self.near[1]:
            copy.wait_recv()
        self.add(self.parts.at[6], (self.parts.at[6], self.landed.at[4], self.landed.at[5]))
        self.over = self.copies.start(self.parts.at[6], self.landed.at[6], self.peer(0, 1))

    def finish(self, store):
        for copy in self.near[0] + [self.over]:
            copy.wait_recv()
        store((self.parts.at[7], self.landed.at[1], self.landed.at[2], self.landed.at[6]))


def summed(refs, where):
    total = refs[0][where].astype(F32)
    for ref in refs[1:]:
        total = total + ref[where].astype(F32)
    return total


def add_rows(step):
    def add(dst, refs):
        def body(i, carry):
            where = (pl.ds(pl.multiple_of(i * step, step), step), slice(None))
            dst[where] = summed(refs, where).astype(dst.dtype)
            return carry

        lax.fori_loop(0, dst.shape[0] // step, body, 0)

    return add


def kernel(
    allowed_ref,
    tok_ref,
    wq_hbm,
    wk_hbm,
    wv_hbm,
    wo_hbm,
    gout_ref,
    att_out,
    dtok_out,
    gq_out,
    gk_out,
    gv_out,
    go_out,
    wq,
    wk,
    wv,
    wo,
    x_all,
    g_all,
    x_sib,
    g_sib,
    xt_all,
    qkv_acc,
    do_acc,
    low,
    pieces,
    cot_pieces,
    kv,
    cots,
    prob,
    mix_acc,
    mix_here,
    mix_in,
    dq_here,
    dq_in,
    mixed,
    mixed_sib,
    grads,
    grads_sib,
    kv_mate,
    kv_mate_in,
    dkv_parts,
    dkv_in,
    att_parts,
    att_in,
    dtok_parts,
    dtok_in,
    wo_parts,
    wo_in,
    wq_parts,
    wq_in,
    wkv_parts,
    wkv_in,
    send_sems,
    recv_sems,
    local_sems,
):
    ctx, tp = lax.axis_index("ctx"), lax.axis_index("tp")
    y, xh, core = ctx // 4, (ctx // 2) % 2, ctx % 2
    z, xl = tp // 2, tp % 2
    width = 512
    half = 256
    scale = HEAD_DIM ** (-0.5)

    def tp_peer(ring, pair):
        return (ctx, ((z + ring) % 4) * 2 + (xl + pair) % 2)

    def tp_at(ring, pair):
        return ((z + ring) % 4) * 2 + (xl + pair) % 2

    def ctx_peer(ring, pair):
        return (((y + ring) % 4) * 4 + ((xh + pair) % 2) * 2 + core, tp)

    def chip_at(ring, pair):
        return ((y + ring) % 4) * 2 + (xh + pair) % 2

    mate = (ctx + 1 - 2 * core, tp)

    local = [
        pltpu.make_async_copy(src, dst, local_sems.at[k])
        for k, (src, dst) in enumerate(
            (
                (tok_ref, x_all.at[tp]),
                (wq_hbm, wq),
                (wk_hbm, wk),
                (wv_hbm, wv),
                (wo_hbm, wo),
                (gout_ref, g_all.at[tp]),
            )
        )
    ]
    for copy in local:
        copy.start()

    barrier = pltpu.get_barrier_semaphore()
    neighbours = [tp_peer(ring, pair) for ring, pair in ((0, 1), (1, 0), (2, 0), (3, 0))]
    neighbours += [ctx_peer(*offset) for offset in ORDER[:7]] + [mate]
    for device in neighbours:
        pl.semaphore_signal(barrier, inc=1, device_id=device, device_id_type=MESH)
    pl.semaphore_wait(barrier, len(neighbours))

    copies = Copies(send_sems, recv_sems)

    def tp_gather(own, slots):
        return Gather(
            copies,
            tp_peer,
            own,
            lambda ring, pair: slots.at[tp_at(ring, pair)],
            lambda to_ring, to_pair, ring, pair: slots.at[tp_at(ring, pair)],
        )

    def turn(ring):
        return (y + ring) % 4

    def exchange(source, target):
        return [
            copies.start(source(turn(ring)), target, ctx_peer(ring, 0)) for ring in (1, 2, 3)
        ]

    def arrived(started):
        for copy in started:
            copy.wait_recv()

    for b in range(2):
        seen = allowed_ref[b, 0]
        for k in range(1, 16):
            seen = seen + allowed_ref[b, k]
        start = (ctx + 1 - seen) * (128 // FRAME)
        low[y, b] = jnp.full((8, 128), start.astype(F32))

    tokens = tp_gather(tok_ref, x_all)
    lows = exchange(lambda to: low.at[y], low.at[y])

    def project(slot, first=False):
        x = x_all[slot]
        rows = pl.ds(pl.multiple_of(slot * width, width), width)
        for k, w in enumerate((wq, wk, wv)):
            term = dot(x, w[rows, :])
            where = (slice(None), slice(k * half, (k + 1) * half))
            if first:
                qkv_acc[where] = term
            else:
                qkv_acc[where] += term

    for copy in local[:4]:
        copy.wait()
    project(tp, first=True)
    tokens.forward_pair()
    project(tp_at(0, 1))
    tokens.forward_far()
    tokens.up.wait_recv()
    tokens.down.wait_recv()
    cotangents = tp_gather(gout_ref, g_all)
    project(tp_at(2, 0))
    project(tp_at(1, 0))
    project(tp_at(3, 0))
    tokens.up_pair.wait_recv()
    tokens.down_pair.wait_recv()
    project(tp_at(1, 1))
    project(tp_at(3, 1))
    tokens.far_pair.wait_recv()
    project(tp_at(2, 1))

    for p in range(4):
        b, h = p // 2, p % 2
        rows = slice(b * 128, (b + 1) * 128)
        for place, which in enumerate((1, 2, 0)):
            at = which * half + h * 128
            pieces[p, place] = qkv_acc[rows, at : at + 128].astype(BF)

    from_side = [
        copies.start(pieces.at[turn(ring), pl.ds(0, 2)], kv.at[y, 0, 1, pl.ds(0, 2)], ctx_peer(ring, 1))
        for ring in range(4)
    ]
    from_rows = exchange(lambda to: pieces.at[to], kv.at[y, 0, 0])
    kv[y, 0, 0] = pieces[y]

    def share(side):
        return copies.start(
            kv.at[:, 0, side, pl.ds(0, 2)], kv.at[:, 1, side, pl.ds(0, 2)], mate
        )

    other_half = pl.ds(pl.multiple_of((1 - core) * half, half), half)
    my_half = pl.ds(pl.multiple_of(core * half, half), half)
    x_half = copies.start(x_all.at[:, :, other_half], x_sib, mate)
    local[5].wait()
    cotangents.forward_pair()
    x_half.wait_recv()

    def transpose_block(k, carry):
        xt_all[k, :, :half] = x_all[k, :, my_half].T
        xt_all[k, :, half:] = x_sib[k].T
        return carry

    lax.fori_loop(0, 8, transpose_block, 0)
    arrived(from_rows)
    shared = [share(0)]
    arrived(from_side)
    shared.append(share(1))
    cotangents.forward_far()
    arrived(shared)
    arrived(lows)

    key_frame = lax.broadcasted_iota(jnp.int32, (128, 128), 0) // FRAME
    frame_gap = key_frame - lax.broadcasted_iota(jnp.int32, (128, 128), 1) // FRAME
    frames = 128 // FRAME
    sides = [(d, side) for d in range(2) for side in range(2)]
    place_of = {
        (d, side): 2 * ((xh + side) % 2) + (core if d == 0 else 1 - core) for d, side in sides
    }
    queries = kv[:, 0, 0, 2].reshape(512, HEAD_DIM)
    batch_here = y // 2
    lowest = jnp.concatenate([low[k, batch_here][0:1] for k in range(4)], axis=1)
    tops = [[] for _ in range(4)]
    for ys in range(4):
        for n, (d, side) in enumerate(sides):
            rows = slice(n * 128, (n + 1) * 128)
            logits = dot_nt(kv[ys, d, side, 0], queries[ys * 128 :]) * scale
            place = place_of[d, side]
            begin = ((4 * ys + place) * frames).astype(F32)
            logits = logits + jnp.where(lowest[:, ys * 128 :] <= begin, 0.0, -jnp.inf)
            ahead = (place_of[0, 0] - place) * frames
            for k in range(ys, 4):
                part = logits[:, (k - ys) * 128 : (k - ys + 1) * 128]
                if k == ys:
                    part = jnp.where(frame_gap <= ahead, part, -jnp.inf)
                prob[ys, rows, k * 128 : (k + 1) * 128] = part
                tops[k].append(jnp.max(part, axis=0, keepdims=True))
    top = jnp.concatenate([functools.reduce(jnp.maximum, t) for t in tops], axis=1)
    totals = [jnp.zeros((1, 128), F32)] * 4
    for ys in range(4):
        for n in range(4):
            rows = slice(n * 128, (n + 1) * 128)
            exponent = jnp.exp(prob[ys, rows, ys * 128 :] - top[:, ys * 128 :])
            prob[ys, rows, ys * 128 :] = exponent
            sums = jnp.sum(exponent, axis=0, keepdims=True)
            for k in range(ys, 4):
                totals[k] = totals[k] + sums[:, (k - ys) * 128 : (k - ys + 1) * 128]
    inverse = 1.0 / jnp.concatenate(totals, axis=1)
    for ys in range(4):
        weights = prob[ys, :, ys * 128 :] * inverse[:, ys * 128 :]
        prob[ys, :, ys * 128 :] = weights
        values = kv[ys, :, :, 1].reshape(512, HEAD_DIM)
        term = dot_tn(weights.astype(BF), values)
        if ys == 0:
            mix_acc[...] = term
        else:
            mix_acc[ys * 128 :] += term
    mix_here[...] = mix_acc[...].astype(BF).reshape(4, 128, HEAD_DIM)
    from_mix = exchange(lambda to: mix_here.at[to], mix_in.at[y])
    mix_in[y] = mix_here[y]
    cotangents.up.wait_recv()
    cotangents.down.wait_recv()
    local[4].wait()

    def pull_back(slot, first=False):
        columns = pl.ds(pl.multiple_of(slot * width, width), width)
        term = dot_nt(g_all[slot], wo[:, columns])
        if first:
            do_acc[...] = term
        else:
            do_acc[...] += term

    pull_back(tp, first=True)
    for offset in ((0, 1), (2, 0), (1, 0), (3, 0)):
        pull_back(tp_at(*offset))
    cotangents.up_pair.wait_recv()
    cotangents.down_pair.wait_recv()
    pull_back(tp_at(1, 1))
    pull_back(tp_at(3, 1))
    cotangents.far_pair.wait_recv()
    pull_back(tp_at(2, 1))
    g_half = copies.start(g_all.at[:, :, other_half], g_sib, mate)
    for p in range(4):
        b, h = p // 2, p % 2
        cot_pieces[p] = do_acc[b * 128 : (b + 1) * 128, h * 128 : (h + 1) * 128].astype(BF)
    from_cots = exchange(lambda to: cot_pieces.at[to], cots.at[y])
    cots[y] = cot_pieces[y]

    def assemble(target, arrivals):
        for p in range(4):
            b, h = p // 2, p % 2
            target[b * 128 : (b + 1) * 128, h * 128 : (h + 1) * 128] = arrivals[p]

    arrived(from_mix)
    assemble(mixed, mix_in)

    mixed_copy = copies.start(mixed, mixed_sib, mate)
    attended = Scatter(copies, tp_peer, att_parts, att_in, add_rows(64))

    def out_part(k):
        columns = pl.ds(pl.multiple_of(tp_at(*ORDER[k]) * width, width), width)
        att_parts[k] = dot(mixed[...], wo[:, columns]).astype(BF)

    for k in range(8):
        out_part(k)
        attended.send(k)
    mixed_copy.wait_recv()
    g_half.wait_recv()

    out_grads = Scatter(copies, ctx_peer, wo_parts, wo_in, add_rows(64))
    for k in range(8):
        chip = chip_at(*ORDER[k])
        wo_parts[k] = (
            dot_tn(mixed[...], g_all[chip, :, my_half]) + dot_tn(mixed_sib[...], g_sib[chip])
        ).astype(BF)
        out_grads.send(k)

    arrived(from_cots)
    cot_rows = cots[...].reshape(512, HEAD_DIM)
    inner = lax.dot_general(
        jnp.ones((8, HEAD_DIM), F32),
        cot_rows.astype(F32) * mix_here[...].reshape(512, HEAD_DIM).astype(F32),
        (((1,), (1,)), ((), ())),
        precision=lax.Precision.HIGHEST,
        preferred_element_type=F32,
    )[0:1]
    mate_copies = []
    for ys in range(4):
        keys = kv[ys, :, :, 0].reshape(512, HEAD_DIM)
        values = kv[ys, :, :, 1].reshape(512, HEAD_DIM)
        weights = prob[ys, :, ys * 128 :]
        slopes = (
            weights * (dot_nt(values, cot_rows[ys * 128 :]) - inner[:, ys * 128 :]) * scale
        ).astype(BF)
        key_part = dot(slopes, queries[ys * 128 :]).astype(BF).reshape(2, 2, 128, HEAD_DIM)
        value_part = (
            dot(weights.astype(BF), cot_rows[ys * 128 :]).astype(BF).reshape(2, 2, 128, HEAD_DIM)
        )
        dkv_parts[ys, :, 0] = key_part[0]
        dkv_parts[ys, :, 1] = value_part[0]
        kv_mate[ys, :, 0] = key_part[1]
        kv_mate[ys, :, 1] = value_part[1]
        mate_copies.append(copies.start(kv_mate.at[ys], kv_mate_in.at[ys], mate))
        term = dot_tn(slopes, keys)
        if ys == 0:
            mix_acc[...] = term
        else:
            mix_acc[ys * 128 :] += term
    dq_here[...] = mix_acc[...].astype(BF).reshape(4, 128, HEAD_DIM)
    from_dq = exchange(lambda to: dq_here.at[to], dq_in.at[y])
    dq_in[y] = dq_here[y]
    for ys in range(4):
        mate_copies[ys].wait_recv()
        for side in range(2):
            dkv_parts[ys, side] = summed((dkv_parts, kv_mate_in), (ys, side)).astype(BF)
    from_dkv = [
        copies.start(dkv_parts.at[turn(ring), side], dkv_in.at[y, side], ctx_peer(ring, side))
        for ring in (2, 1, 3, 0)
        for side in (1, 0)
        if (ring, side) != (0, 0)
    ]
    dkv_in[y, 0] = dkv_parts[y, 0]
    arrived(from_dq)
    assemble(grads, dq_in)
    dq_copy = copies.start(grads.at[:, pl.ds(0, half)], grads_sib.at[:, pl.ds(0, half)], mate)
    attended.relay()
    out_grads.relay()

    dq_copy.wait_recv()
    query_grads = Scatter(copies, ctx_peer, wq_parts, wq_in, add_rows(64))
    for k in range(8):
        chip = chip_at(*ORDER[k])
        wq_parts[k] = (
            dot(xt_all[chip, :, :half], grads[:, :half])
            + dot(xt_all[chip, :, half:], grads_sib[:, :half])
        ).astype(BF)
        query_grads.send(k)

    def store_rows(out):
        return lambda refs: add_rows(64)(out, refs)

    arrived(from_dkv)
    for p in range(4):
        b, h = p // 2, p % 2
        for which in range(2):
            at = (1 + which) * half + h * 128
            grads[b * 128 : (b + 1) * 128, at : at + 128] = summed(
                (dkv_in.at[:, 0], dkv_in.at[:, 1]), (p, which)
            ).astype(BF)
    kv_columns = pl.ds(half, 2 * half)
    dkv_copy = copies.start(grads.at[:, kv_columns], grads_sib.at[:, kv_columns], mate)
    query_grads.relay()
    attended.cross()
    out_grads.cross()

    token_grads = Scatter(copies, tp_peer, dtok_parts, dtok_in, add_rows(64))
    for k in range(8):
        rows = pl.ds(pl.multiple_of(tp_at(*ORDER[k]) * width, width), width)
        dtok_parts[k] = (
            dot_nt(grads[:, :half], wq[rows, :])
            + dot_nt(grads[:, half : 2 * half], wk[rows, :])
            + dot_nt(grads[:, 2 * half :], wv[rows, :])
        ).astype(BF)
        token_grads.send(k)

    dkv_copy.wait_recv()
    kv_grads = Scatter(copies, ctx_peer, wkv_parts, wkv_in, add_rows(64))
    for k in range(8):
        chip = chip_at(*ORDER[k])
        wkv_parts[k] = (
            dot(xt_all[chip, :, :half], grads[:, half:])
            + dot(xt_all[chip, :, half:], grads_sib[:, half:])
        ).astype(BF)
        kv_grads.send(k)
    query_grads.cross()
    token_grads.relay()
    kv_grads.relay()
    attended.finish(store_rows(att_out))
    out_grads.finish(store_rows(go_out))
    token_grads.cross()
    kv_grads.cross()
    query_grads.finish(store_rows(gq_out))
    token_grads.finish(store_rows(dtok_out))

    def store_pair(refs):
        def body(i, carry):
            rows = pl.ds(pl.multiple_of(i * 64, 64), 64)
            total = summed(refs, (rows, slice(None))).astype(BF)
            gk_out[rows, :] = total[:, :half]
            gv_out[rows, :] = total[:, half:]
            return carry

        lax.fori_loop(0, 4, body, 0)

    kv_grads.finish(store_pair)
    copies.finish()


def settle(*refs):
    sources, results, held, sems = refs[:6], refs[6:12], refs[12:18], refs[18]
    reads = [pltpu.make_async_copy(sources[k], held[k], sems.at[k]) for k in range(6)]
    writes = [pltpu.make_async_copy(held[k], results[k], sems.at[6 + k]) for k in range(6)]
    for read in reads:
        read.start()
    for read, write in zip(reads, writes):
        read.wait()
        write.start()
    for write in writes:
        write.wait()


N_COPIES = 2 * GATHER_COPIES + 5 * SCATTER_COPIES + 26 + 2 + 4 + 5


def per_device(tokens, w_query, w_key, w_value, w_out, allowed, grad_out):
    batch, block, width = tokens.shape
    rows = batch * block
    head_width = w_query.shape[1]
    vmem = pl.BlockSpec(memory_space=pltpu.VMEM)
    hbm = pl.BlockSpec(memory_space=pl.ANY)

    def halves(*shape):
        return pltpu.VMEM(shape, BF)

    def pair(*shape):
        return [halves(8, *shape), halves(7, *shape)]

    outs = pl.pallas_call(
        kernel,
        out_shape=[jax.ShapeDtypeStruct((rows, width), BF)] * 2
        + [jax.ShapeDtypeStruct((head_width, head_width), BF)] * 4,
        in_specs=[pl.BlockSpec(memory_space=pltpu.SMEM)] + [hbm] * 6,
        out_specs=[vmem] * 6,
        scratch_shapes=[
            halves(4096, 256),
            halves(4096, 256),
            halves(4096, 256),
            halves(256, 4096),
            halves(8, 256, 512),
            halves(8, 256, 512),
            halves(8, 256, 256),
            halves(8, 256, 256),
            halves(8, 256, 512),
            pltpu.VMEM((256, 768), F32),
            pltpu.VMEM((256, 256), F32),
            pltpu.VMEM((4, 2, 8, 128), F32),
            halves(4, 3, 128, 128),
            halves(4, 128, 128),
            halves(4, 2, 2, 3, 128, 128),
            halves(4, 128, 128),
            pltpu.VMEM((4, 512, 512), F32),
            pltpu.VMEM((512, 128), F32),
            halves(4, 128, 128),
            halves(4, 128, 128),
            halves(4, 128, 128),
            halves(4, 128, 128),
            halves(256, 256),
            halves(256, 256),
            halves(256, 768),
            halves(256, 768),
            halves(4, 2, 2, 128, 128),
            halves(4, 2, 2, 128, 128),
            halves(4, 2, 2, 128, 128),
            halves(4, 2, 2, 128, 128),
            *pair(256, 512),
            *pair(256, 512),
            *pair(256, 256),
            *pair(256, 256),
            *pair(256, 512),
            pltpu.SemaphoreType.DMA((N_COPIES,)),
            pltpu.SemaphoreType.DMA((N_COPIES,)),
            pltpu.SemaphoreType.DMA((6,)),
        ],
        compiler_params=pltpu.CompilerParams(
            collective_id=0, has_side_effects=True, vmem_limit_bytes=60 * 2**20
        ),
    )(
        allowed.reshape(batch, allowed.shape[2]),
        tokens.reshape(rows, width),
        w_query,
        w_key,
        w_value,
        w_out,
        grad_out.reshape(rows, width),
    )
    attended, grad_tokens, *weight_grads = pl.pallas_call(
        settle,
        out_shape=[jax.ShapeDtypeStruct(out.shape, out.dtype) for out in outs],
        in_specs=[hbm] * 6,
        out_specs=[hbm] * 6,
        scratch_shapes=[pltpu.VMEM(out.shape, out.dtype) for out in outs]
        + [pltpu.SemaphoreType.DMA((12,))],
    )(*outs)
    return (
        attended.reshape(batch, block, width),
        grad_tokens.reshape(batch, block, width),
        *weight_grads,
    )


def solution(mesh):
    placed = (
        P(None, "ctx", "tp"),
        P(None, "tp"),
        P(None, "tp"),
        P(None, "tp"),
        P("tp", None),
        P(None, "ctx", None),
        P(None, "ctx", "tp"),
    )
    return jax.shard_map(
        per_device,
        mesh=mesh,
        in_specs=placed,
        out_specs=(
            P(None, "ctx", "tp"),
            P(None, "ctx", "tp"),
            P("ctx", "tp"),
            P("ctx", "tp"),
            P("ctx", "tp"),
            P("tp", "ctx"),
        ),
        check_vma=False,
    )
```

```python
import functools

import jax
import jax.numpy as jnp
from jax import lax
from jax.experimental import pallas as pl
from jax.experimental.pallas import tpu as pltpu
from jax.sharding import PartitionSpec as P

HEAD_DIM = 128
FRAME = 16
MESH = pl.DeviceIdType.MESH
BF = jnp.bfloat16
F32 = jnp.float32

ORDER = ((2, 1), (1, 1), (3, 1), (2, 0), (1, 0), (3, 0), (0, 1), (0, 0))
GATHER_COPIES = 7
SCATTER_COPIES = 13


def dot(a, b):
    return jnp.dot(a, b, preferred_element_type=F32)


def dot_nt(a, b):
    return lax.dot_general(a, b, (((1,), (1,)), ((), ())), preferred_element_type=F32)


def dot_tn(a, b):
    return lax.dot_general(a, b, (((0,), (0,)), ((), ())), preferred_element_type=F32)


class Copies:
    def __init__(self, send_sems, recv_sems):
        self.send_sems, self.recv_sems = send_sems, recv_sems
        self.used = 0
        self.started = []

    def start(self, src, dst, device):
        k = self.used
        self.used += 1
        copy = pltpu.make_async_remote_copy(
            src_ref=src,
            dst_ref=dst,
            send_sem=self.send_sems.at[k],
            recv_sem=self.recv_sems.at[k],
            device_id=device,
            device_id_type=MESH,
        )
        copy.start()
        self.started.append(copy)
        return copy

    def finish(self):
        for copy in self.started:
            copy.wait_send()


class Gather:
    def __init__(self, copies, peer, own, slot, landing):
        self.copies, self.peer, self.slot, self.landing = copies, peer, slot, landing
        go = copies.start
        self.pair = go(own, landing(0, 1, 0, 0), peer(0, 1))
        self.far = go(own, landing(2, 0, 0, 0), peer(2, 0))
        self.up = go(own, landing(1, 0, 0, 0), peer(1, 0))
        self.down = go(own, landing(3, 0, 0, 0), peer(3, 0))

    def forward_pair(self):
        self.pair.wait_recv()
        go = self.copies.start
        self.up_pair = go(self.slot(0, 1), self.landing(1, 0, 0, 1), self.peer(1, 0))
        self.down_pair = go(self.slot(0, 1), self.landing(3, 0, 0, 1), self.peer(3, 0))

    def forward_far(self):
        self.far.wait_recv()
        self.far_pair = self.copies.start(
            self.slot(2, 0), self.landing(0, 1, 2, 0), self.peer(0, 1)
        )


class Scatter:
    def __init__(self, copies, peer, parts, landed, add):
        self.copies, self.peer, self.parts, self.landed, self.add = copies, peer, parts, landed, add
        rows = parts.shape[1] // 2
        self.low, self.high = pl.ds(0, rows), pl.ds(rows, rows)
        self.far, self.near = [[], []], [[], []]

    def move(self, k, slot, rows, ring):
        return self.copies.start(
            self.parts.at[k, rows], self.landed.at[slot, rows], self.peer(ring, 0)
        )

    def send(self, k):
        if k >= 6:
            return
        ring, pair = ORDER[k]
        slot = 3 * pair
        if ring == 2:
            self.far[pair] = [self.move(k, slot, self.low, 1), self.move(k, slot, self.high, 3)]
        elif ring == 1:
            self.near[pair].append(self.move(k, slot + 1, self.high, 1))
        else:
            self.near[pair].append(self.move(k, slot + 2, self.low, 3))

    def relay(self):
        for pair in (1, 0):
            first, slot = 3 - 3 * pair, 3 * pair
            for copy, k, to, rows, ring in (
                (self.far[pair][0], first + 1, slot + 1, self.low, 1),
                (self.far[pair][1], first + 2, slot + 2, self.high, 3),
            ):
                copy.wait_recv()
                part = self.parts.at[k, rows]
                self.add(part, (part, self.landed.at[slot, rows]))
                self.near[pair].append(self.move(k, to, rows, ring))

    def cross(self):
        for copy in self.near[1]:
            copy.wait_recv()
        self.add(self.parts.at[6], (self.parts.at[6], self.landed.at[4], self.landed.at[5]))
        self.over = self.copies.start(self.parts.at[6], self.landed.at[6], self.peer(0, 1))

    def finish(self, store):
        for copy in self.near[0] + [self.over]:
            copy.wait_recv()
        store((self.parts.at[7], self.landed.at[1], self.landed.at[2], self.landed.at[6]))


def summed(refs, where):
    total = refs[0][where].astype(F32)
    for ref in refs[1:]:
        total = total + ref[where].astype(F32)
    return total


def add_rows(step):
    def add(dst, refs):
        for at in range(0, dst.shape[0], step):
            where = (pl.ds(at, step), slice(None))
            dst[where] = summed(refs, where).astype(dst.dtype)

    return add


def kernel(
    allowed_ref,
    tok_ref,
    wq_hbm,
    wk_hbm,
    wv_hbm,
    wo_hbm,
    gout_ref,
    att_out,
    dtok_out,
    gq_out,
    gk_out,
    gv_out,
    go_out,
    wq,
    wk,
    wv,
    wo,
    x_all,
    g_all,
    x_sib,
    g_sib,
    xt_all,
    qkv_acc,
    do_acc,
    low,
    pieces,
    cot_pieces,
    kv,
    cots,
    prob,
    mix_acc,
    mix_here,
    mix_in,
    dq_here,
    dq_in,
    mixed,
    mixed_sib,
    grads,
    grads_sib,
    kv_mate,
    kv_mate_in,
    dkv_parts,
    dkv_in,
    att_parts,
    att_in,
    dtok_parts,
    dtok_in,
    wo_parts,
    wo_in,
    wq_parts,
    wq_in,
    wkv_parts,
    wkv_in,
    send_sems,
    recv_sems,
    local_sems,
):
    ctx, tp = lax.axis_index("ctx"), lax.axis_index("tp")
    y, xh, core = ctx // 4, (ctx // 2) % 2, ctx % 2
    z, xl = tp // 2, tp % 2
    width = 512
    half = 256
    scale = HEAD_DIM ** (-0.5)

    def tp_peer(ring, pair):
        return (ctx, ((z + ring) % 4) * 2 + (xl + pair) % 2)

    def tp_at(ring, pair):
        return ((z + ring) % 4) * 2 + (xl + pair) % 2

    def ctx_peer(ring, pair):
        return (((y + ring) % 4) * 4 + ((xh + pair) % 2) * 2 + core, tp)

    def chip_at(ring, pair):
        return ((y + ring) % 4) * 2 + (xh + pair) % 2

    mate = (ctx + 1 - 2 * core, tp)

    local = [
        pltpu.make_async_copy(src, dst, local_sems.at[k])
        for k, (src, dst) in enumerate(
            (
                (tok_ref, x_all.at[tp]),
                (wq_hbm, wq),
                (wk_hbm, wk),
                (wv_hbm, wv),
                (wo_hbm, wo),
                (gout_ref, g_all.at[tp]),
            )
        )
    ]
    for copy in local:
        copy.start()

    barrier = pltpu.get_barrier_semaphore()
    neighbours = [tp_peer(ring, pair) for ring, pair in ((0, 1), (1, 0), (2, 0), (3, 0))]
    neighbours += [ctx_peer(*offset) for offset in ORDER[:7]] + [mate]
    for device in neighbours:
        pl.semaphore_signal(barrier, inc=1, device_id=device, device_id_type=MESH)
    pl.semaphore_wait(barrier, len(neighbours))

    copies = Copies(send_sems, recv_sems)

    def tp_gather(own, slots):
        return Gather(
            copies,
            tp_peer,
            own,
            lambda ring, pair: slots.at[tp_at(ring, pair)],
            lambda to_ring, to_pair, ring, pair: slots.at[tp_at(ring, pair)],
        )

    def turn(ring):
        return (y + ring) % 4

    def exchange(source, target):
        return [
            copies.start(source(turn(ring)), target, ctx_peer(ring, 0)) for ring in (1, 2, 3)
        ]

    def arrived(started):
        for copy in started:
            copy.wait_recv()

    for b in range(2):
        seen = allowed_ref[b, 0]
        for k in range(1, 16):
            seen = seen + allowed_ref[b, k]
        start = (ctx + 1 - seen) * (128 // FRAME)
        low[y, b] = jnp.full((8, 128), start.astype(F32))

    tokens = tp_gather(tok_ref, x_all)
    lows = exchange(lambda to: low.at[y], low.at[y])

    def project(slot, first=False):
        x = x_all[slot]
        rows = pl.ds(pl.multiple_of(slot * width, width), width)
        for k, w in enumerate((wq, wk, wv)):
            term = dot(x, w[rows, :])
            where = (slice(None), slice(k * half, (k + 1) * half))
            if first:
                qkv_acc[where] = term
            else:
                qkv_acc[where] += term

    for copy in local[:4]:
        copy.wait()
    project(tp, first=True)
    tokens.forward_pair()
    cotangents = tp_gather(gout_ref, g_all)
    project(tp_at(0, 1))
    tokens.forward_far()
    tokens.up.wait_recv()
    tokens.down.wait_recv()
    project(tp_at(2, 0))
    project(tp_at(1, 0))
    project(tp_at(3, 0))
    tokens.up_pair.wait_recv()
    tokens.down_pair.wait_recv()
    project(tp_at(1, 1))
    project(tp_at(3, 1))
    tokens.far_pair.wait_recv()
    project(tp_at(2, 1))

    for p in range(4):
        b, h = p // 2, p % 2
        rows = slice(b * 128, (b + 1) * 128)
        for place, which in enumerate((1, 2, 0)):
            at = which * half + h * 128
            pieces[p, place] = qkv_acc[rows, at : at + 128].astype(BF)

    from_side = [
        copies.start(pieces.at[turn(ring), pl.ds(0, 2)], kv.at[y, 0, 1, pl.ds(0, 2)], ctx_peer(ring, 1))
        for ring in range(4)
    ]
    from_rows = exchange(lambda to: pieces.at[to], kv.at[y, 0, 0])
    kv[y, 0, 0] = pieces[y]

    def share(side):
        return copies.start(
            kv.at[:, 0, side, pl.ds(0, 2)], kv.at[:, 1, side, pl.ds(0, 2)], mate
        )

    other_half = pl.ds(pl.multiple_of((1 - core) * half, half), half)
    my_half = pl.ds(pl.multiple_of(core * half, half), half)
    x_half = copies.start(x_all.at[:, :, other_half], x_sib, mate)
    local[5].wait()
    cotangents.forward_pair()
    x_half.wait_recv()

    def transpose_block(k, carry):
        xt_all[k, :, :half] = x_all[k, :, my_half].T
        xt_all[k, :, half:] = x_sib[k].T
        return carry

    lax.fori_loop(0, 8, transpose_block, 0)
    arrived(from_rows)
    shared = [share(0)]
    arrived(from_side)
    shared.append(share(1))
    cotangents.forward_far()
    arrived(shared)
    arrived(lows)

    key_frame = lax.broadcasted_iota(jnp.int32, (128, 128), 0) // FRAME
    frame_gap = key_frame - lax.broadcasted_iota(jnp.int32, (128, 128), 1) // FRAME
    frames = 128 // FRAME
    sides = [(d, side) for d in range(2) for side in range(2)]
    place_of = {
        (d, side): 2 * ((xh + side) % 2) + (core if d == 0 else 1 - core) for d, side in sides
    }
    queries = kv[:, 0, 0, 2].reshape(512, HEAD_DIM)
    batch_here = y // 2
    lowest = jnp.concatenate([low[k, batch_here][0:1] for k in range(4)], axis=1)
    tops = [[] for _ in range(4)]
    for ys in range(4):
        for n, (d, side) in enumerate(sides):
            rows = slice(n * 128, (n + 1) * 128)
            logits = dot_nt(kv[ys, d, side, 0], queries[ys * 128 :]) * scale
            place = place_of[d, side]
            begin = ((4 * ys + place) * frames).astype(F32)
            logits = logits + jnp.where(lowest[:, ys * 128 :] <= begin, 0.0, -jnp.inf)
            ahead = (place_of[0, 0] - place) * frames
            for k in range(ys, 4):
                part = logits[:, (k - ys) * 128 : (k - ys + 1) * 128]
                if k == ys:
                    part = jnp.where(frame_gap <= ahead, part, -jnp.inf)
                prob[ys, rows, k * 128 : (k + 1) * 128] = part
                tops[k].append(jnp.max(part, axis=0, keepdims=True))
    top = jnp.concatenate([functools.reduce(jnp.maximum, t) for t in tops], axis=1)
    totals = [jnp.zeros((1, 128), F32)] * 4
    for ys in range(4):
        for n in range(4):
            rows = slice(n * 128, (n + 1) * 128)
            exponent = jnp.exp(prob[ys, rows, ys * 128 :] - top[:, ys * 128 :])
            prob[ys, rows, ys * 128 :] = exponent
            sums = jnp.sum(exponent, axis=0, keepdims=True)
            for k in range(ys, 4):
                totals[k] = totals[k] + sums[:, (k - ys) * 128 : (k - ys + 1) * 128]
    inverse = 1.0 / jnp.concatenate(totals, axis=1)
    for ys in range(4):
        weights = prob[ys, :, ys * 128 :] * inverse[:, ys * 128 :]
        prob[ys, :, ys * 128 :] = weights
        values = kv[ys, :, :, 1].reshape(512, HEAD_DIM)
        term = dot_tn(weights.astype(BF), values)
        if ys == 0:
            mix_acc[...] = term
        else:
            mix_acc[ys * 128 :] += term
    mix_here[...] = mix_acc[...].astype(BF).reshape(4, 128, HEAD_DIM)
    from_mix = exchange(lambda to: mix_here.at[to], mix_in.at[y])
    mix_in[y] = mix_here[y]
    cotangents.up.wait_recv()
    cotangents.down.wait_recv()
    local[4].wait()

    def pull_back(slot, first=False):
        columns = pl.ds(pl.multiple_of(slot * width, width), width)
        term = dot_nt(g_all[slot], wo[:, columns])
        if first:
            do_acc[...] = term
        else:
            do_acc[...] += term

    pull_back(tp, first=True)
    for offset in ((0, 1), (2, 0), (1, 0), (3, 0)):
        pull_back(tp_at(*offset))
    cotangents.up_pair.wait_recv()
    cotangents.down_pair.wait_recv()
    pull_back(tp_at(1, 1))
    pull_back(tp_at(3, 1))
    cotangents.far_pair.wait_recv()
    pull_back(tp_at(2, 1))
    g_half = copies.start(g_all.at[:, :, other_half], g_sib, mate)
    for p in range(4):
        b, h = p // 2, p % 2
        cot_pieces[p] = do_acc[b * 128 : (b + 1) * 128, h * 128 : (h + 1) * 128].astype(BF)
    from_cots = exchange(lambda to: cot_pieces.at[to], cots.at[y])
    cots[y] = cot_pieces[y]

    def assemble(target, arrivals):
        for p in range(4):
            b, h = p // 2, p % 2
            target[b * 128 : (b + 1) * 128, h * 128 : (h + 1) * 128] = arrivals[p]

    arrived(from_mix)
    assemble(mixed, mix_in)

    mixed_copy = copies.start(mixed, mixed_sib, mate)
    attended = Scatter(copies, tp_peer, att_parts, att_in, add_rows(64))

    def out_part(k):
        columns = pl.ds(pl.multiple_of(tp_at(*ORDER[k]) * width, width), width)
        att_parts[k] = dot(mixed[...], wo[:, columns]).astype(BF)

    for k in range(8):
        out_part(k)
        attended.send(k)
    mixed_copy.wait_recv()
    g_half.wait_recv()

    out_grads = Scatter(copies, ctx_peer, wo_parts, wo_in, add_rows(64))
    for k in range(8):
        chip = chip_at(*ORDER[k])
        wo_parts[k] = (
            dot_tn(mixed[...], g_all[chip, :, my_half]) + dot_tn(mixed_sib[...], g_sib[chip])
        ).astype(BF)
        out_grads.send(k)

    arrived(from_cots)
    cot_rows = cots[...].reshape(512, HEAD_DIM)
    inner = lax.dot_general(
        jnp.ones((8, HEAD_DIM), F32),
        cot_rows.astype(F32) * mix_here[...].reshape(512, HEAD_DIM).astype(F32),
        (((1,), (1,)), ((), ())),
        precision=lax.Precision.HIGHEST,
        preferred_element_type=F32,
    )[0:1]
    mate_copies = []
    for ys in range(4):
        keys = kv[ys, :, :, 0].reshape(512, HEAD_DIM)
        values = kv[ys, :, :, 1].reshape(512, HEAD_DIM)
        weights = prob[ys, :, ys * 128 :]
        slopes = (
            weights * (dot_nt(values, cot_rows[ys * 128 :]) - inner[:, ys * 128 :]) * scale
        ).astype(BF)
        key_part = dot(slopes, queries[ys * 128 :]).astype(BF).reshape(2, 2, 128, HEAD_DIM)
        value_part = (
            dot(weights.astype(BF), cot_rows[ys * 128 :]).astype(BF).reshape(2, 2, 128, HEAD_DIM)
        )
        dkv_parts[ys, :, 0] = key_part[0]
        dkv_parts[ys, :, 1] = value_part[0]
        kv_mate[ys, :, 0] = key_part[1]
        kv_mate[ys, :, 1] = value_part[1]
        mate_copies.append(copies.start(kv_mate.at[ys], kv_mate_in.at[ys], mate))
        term = dot_tn(slopes, keys)
        if ys == 0:
            mix_acc[...] = term
        else:
            mix_acc[ys * 128 :] += term
    dq_here[...] = mix_acc[...].astype(BF).reshape(4, 128, HEAD_DIM)
    from_dq = exchange(lambda to: dq_here.at[to], dq_in.at[y])
    dq_in[y] = dq_here[y]
    for ys in range(4):
        mate_copies[ys].wait_recv()
        for side in range(2):
            dkv_parts[ys, side] = summed((dkv_parts, kv_mate_in), (ys, side)).astype(BF)
    from_dkv = [
        copies.start(dkv_parts.at[turn(ring), side], dkv_in.at[y, side], ctx_peer(ring, side))
        for ring in (2, 1, 3, 0)
        for side in (1, 0)
        if (ring, side) != (0, 0)
    ]
    dkv_in[y, 0] = dkv_parts[y, 0]
    arrived(from_dq)
    assemble(grads, dq_in)
    dq_copy = copies.start(grads.at[:, pl.ds(0, half)], grads_sib.at[:, pl.ds(0, half)], mate)
    attended.relay()
    out_grads.relay()

    dq_copy.wait_recv()
    query_grads = Scatter(copies, ctx_peer, wq_parts, wq_in, add_rows(64))
    for k in range(8):
        chip = chip_at(*ORDER[k])
        wq_parts[k] = (
            dot(xt_all[chip, :, :half], grads[:, :half])
            + dot(xt_all[chip, :, half:], grads_sib[:, :half])
        ).astype(BF)
        query_grads.send(k)

    def store_rows(out):
        return lambda refs: add_rows(64)(out, refs)

    arrived(from_dkv)
    for p in range(4):
        b, h = p // 2, p % 2
        for which in range(2):
            at = (1 + which) * half + h * 128
            grads[b * 128 : (b + 1) * 128, at : at + 128] = summed(
                (dkv_in.at[:, 0], dkv_in.at[:, 1]), (p, which)
            ).astype(BF)
    kv_columns = pl.ds(half, 2 * half)
    dkv_copy = copies.start(grads.at[:, kv_columns], grads_sib.at[:, kv_columns], mate)
    query_grads.relay()
    attended.cross()
    out_grads.cross()

    token_grads = Scatter(copies, tp_peer, dtok_parts, dtok_in, add_rows(64))
    for k in range(8):
        rows = pl.ds(pl.multiple_of(tp_at(*ORDER[k]) * width, width), width)
        dtok_parts[k] = (
            dot_nt(grads[:, :half], wq[rows, :])
            + dot_nt(grads[:, half : 2 * half], wk[rows, :])
            + dot_nt(grads[:, 2 * half :], wv[rows, :])
        ).astype(BF)
        token_grads.send(k)

    dkv_copy.wait_recv()
    kv_grads = Scatter(copies, ctx_peer, wkv_parts, wkv_in, add_rows(64))
    for k in range(8):
        chip = chip_at(*ORDER[k])
        wkv_parts[k] = (
            dot(xt_all[chip, :, :half], grads[:, half:])
            + dot(xt_all[chip, :, half:], grads_sib[:, half:])
        ).astype(BF)
        kv_grads.send(k)
    attended.finish(store_rows(att_out))
    out_grads.finish(store_rows(go_out))
    token_grads.relay()
    query_grads.cross()
    kv_grads.relay()
    token_grads.cross()
    kv_grads.cross()
    query_grads.finish(store_rows(gq_out))
    token_grads.finish(store_rows(dtok_out))

    def store_pair(refs):
        def body(i, carry):
            rows = pl.ds(pl.multiple_of(i * 64, 64), 64)
            total = summed(refs, (rows, slice(None))).astype(BF)
            gk_out[rows, :] = total[:, :half]
            gv_out[rows, :] = total[:, half:]
            return carry

        lax.fori_loop(0, 4, body, 0)

    kv_grads.finish(store_pair)
    copies.finish()


def settle(*refs):
    sources, results, held, sems = refs[:6], refs[6:12], refs[12:18], refs[18]
    reads = [pltpu.make_async_copy(sources[k], held[k], sems.at[k]) for k in range(6)]
    writes = [pltpu.make_async_copy(held[k], results[k], sems.at[6 + k]) for k in range(6)]
    for read in reads:
        read.start()
    for read, write in zip(reads, writes):
        read.wait()
        write.start()
    for write in writes:
        write.wait()


N_COPIES = 2 * GATHER_COPIES + 5 * SCATTER_COPIES + 26 + 2 + 4 + 5


def per_device(tokens, w_query, w_key, w_value, w_out, allowed, grad_out):
    batch, block, width = tokens.shape
    rows = batch * block
    head_width = w_query.shape[1]
    vmem = pl.BlockSpec(memory_space=pltpu.VMEM)
    hbm = pl.BlockSpec(memory_space=pl.ANY)

    def halves(*shape):
        return pltpu.VMEM(shape, BF)

    def pair(*shape):
        return [halves(8, *shape), halves(7, *shape)]

    outs = pl.pallas_call(
        kernel,
        out_shape=[jax.ShapeDtypeStruct((rows, width), BF)] * 2
        + [jax.ShapeDtypeStruct((head_width, head_width), BF)] * 4,
        in_specs=[pl.BlockSpec(memory_space=pltpu.SMEM)] + [hbm] * 6,
        out_specs=[vmem] * 6,
        scratch_shapes=[
            halves(4096, 256),
            halves(4096, 256),
            halves(4096, 256),
            halves(256, 4096),
            halves(8, 256, 512),
            halves(8, 256, 512),
            halves(8, 256, 256),
            halves(8, 256, 256),
            halves(8, 256, 512),
            pltpu.VMEM((256, 768), F32),
            pltpu.VMEM((256, 256), F32),
            pltpu.VMEM((4, 2, 8, 128), F32),
            halves(4, 3, 128, 128),
            halves(4, 128, 128),
            halves(4, 2, 2, 3, 128, 128),
            halves(4, 128, 128),
            pltpu.VMEM((4, 512, 512), F32),
            pltpu.VMEM((512, 128), F32),
            halves(4, 128, 128),
            halves(4, 128, 128),
            halves(4, 128, 128),
            halves(4, 128, 128),
            halves(256, 256),
            halves(256, 256),
            halves(256, 768),
            halves(256, 768),
            halves(4, 2, 2, 128, 128),
            halves(4, 2, 2, 128, 128),
            halves(4, 2, 2, 128, 128),
            halves(4, 2, 2, 128, 128),
            *pair(256, 512),
            *pair(256, 512),
            *pair(256, 256),
            *pair(256, 256),
            *pair(256, 512),
            pltpu.SemaphoreType.DMA((N_COPIES,)),
            pltpu.SemaphoreType.DMA((N_COPIES,)),
            pltpu.SemaphoreType.DMA((6,)),
        ],
        compiler_params=pltpu.CompilerParams(
            collective_id=0, has_side_effects=True, vmem_limit_bytes=60 * 2**20
        ),
    )(
        allowed.reshape(batch, allowed.shape[2]),
        tokens.reshape(rows, width),
        w_query,
        w_key,
        w_value,
        w_out,
        grad_out.reshape(rows, width),
    )
    attended, grad_tokens, *weight_grads = pl.pallas_call(
        settle,
        out_shape=[jax.ShapeDtypeStruct(out.shape, out.dtype) for out in outs],
        in_specs=[hbm] * 6,
        out_specs=[hbm] * 6,
        scratch_shapes=[pltpu.VMEM(out.shape, out.dtype) for out in outs]
        + [pltpu.SemaphoreType.DMA((12,))],
    )(*outs)
    return (
        attended.reshape(batch, block, width),
        grad_tokens.reshape(batch, block, width),
        *weight_grads,
    )


def solution(mesh):
    placed = (
        P(None, "ctx", "tp"),
        P(None, "tp"),
        P(None, "tp"),
        P(None, "tp"),
        P("tp", None),
        P(None, "ctx", None),
        P(None, "ctx", "tp"),
    )
    return jax.shard_map(
        per_device,
        mesh=mesh,
        in_specs=placed,
        out_specs=(
            P(None, "ctx", "tp"),
            P(None, "ctx", "tp"),
            P("ctx", "tp"),
            P("ctx", "tp"),
            P("ctx", "tp"),
            P("tp", "ctx"),
        ),
        check_vma=False,
    )
```
